512 devices in a mesh: wide: 64 (over y, z), narrow: 8 (over x, core).
Axes of the slice: x: 4, y: 8, z: 8, core: 2. Of those that a mesh axis runs over, the one named last changes fastest.
Arguments:
- item_states: bfloat16 [65536, 2048], P(('wide', 'narrow'))
- item_gain: bfloat16 [2048], replicated, may hold values from 0.5 to 1.5
- wq_item: bfloat16 [2048, 2048], P(None, 'narrow')
- wkv_item: bfloat16 [2048, 8, 128], P(None, 'narrow')
- wo_item: bfloat16 [2048, 2048], P('narrow'), may hold values from -0.125 to 0.125
- user_gain: bfloat16 [2048], replicated, may hold values from 0.5 to 1.5
- wq_user: bfloat16 [2048, 2048], P('wide', 'narrow')
- wkv_user: bfloat16 [2048, 8, 128], P('wide', 'narrow')
- wo_user: bfloat16 [2048, 2048], P('narrow', 'wide'), may hold values from -0.125 to 0.125
- history_items: int32 [64, 512], P('wide'), may hold values from 0 to 511, as said below
- history_lengths: int32 [64], P('wide'), may hold values from 1 to 512, 16384 in all
Outputs:
- item_embeddings: bfloat16 [512, 2048], P('wide', 'narrow')
- user_states: bfloat16 [32768, 2048], P('wide', 'narrow')
The draws below stay inside these ranges and needn't reach their ends.
Inputs may be any that keep to these rules, and one draw needn't show every extreme that they name: `history_items`: every user's history names at most 16 slots of items whose ids lie in one run of 8 ids (k * 8 to (k + 1) * 8 - 1), and exactly 16 for some run.
All inputs are finite; a program needn't handle non-finite values. No bound on the sum of `history_lengths` on one device may be relied on, other than what follows from the above.
Results may differ from the reference program's by a relative error of at most 0.0065.
Values may be sent and summed in bfloat16 or wider, within the bound.
No kernel may reach another device: no remote copies, remote signals or barrier semaphores. Data moves between devices by JAX's collectives and lax.ppermute only.
A program may use at most 64 MiB of HBM per device.

```python
import math
import jax
import jax.numpy as jnp
import numpy as np
from jax import lax

D = 2048
HEADS = 32
KV_HEADS = 8
HEAD_DIM = 64
TXT = 128
HMAX = 512
ITEM_GRP = 8
ITEMS = 512
CAP = 16
ROWS = 32768
N_WIDE = 64


def kv_base(key, salt):
    return jax.random.normal(jax.random.fold_in(key, salt), (D, KV_HEADS, 2 * HEAD_DIM), jnp.float32) * D ** (-0.5)


def draw_item_states(key, part):
    key = jax.random.fold_in(key, 3)
    first, second, third = jax.random.split(key, 3)
    columns = jnp.exp(jax.random.uniform(second, (D,), jnp.float32, 0.0, math.log(10.0)))
    rows = jnp.exp(jax.random.uniform(third, (ITEMS * TXT, 1), jnp.float32, 0.0, math.log(10.0)))
    base = jax.random.normal(first, (ITEMS * TXT, D), jnp.float32)
    return (base * columns[None, :] * rows / 5.0).astype(jnp.bfloat16)


def draw_wkv_item(key, part):
    return kv_base(key, 11).astype(jnp.bfloat16)


def draw_wkv_user(key, part):
    return kv_base(key, 12).astype(jnp.bfloat16)


def draw_wq_item(key, part):
    key = jax.random.fold_in(key, 21)
    first = jax.random.fold_in(key, 0)
    fresh = jax.random.normal(first, (D, HEADS * HEAD_DIM), jnp.float32) * D ** (-0.5)
    return fresh.astype(jnp.bfloat16)


def draw_wq_user(key, part):
    key = jax.random.fold_in(key, 22)
    first = jax.random.fold_in(key, 0)
    fresh = jax.random.normal(first, (D, HEADS * HEAD_DIM), jnp.float32) * D ** (-0.5)
    return fresh.astype(jnp.bfloat16)


def draw_history_items(key, part):
    key = jax.random.fold_in(key, 5)
    tickets = N_WIDE * CAP

    def one_user(user_key):
        first, second, third, fourth = jax.random.split(user_key, 4)
        score = jax.random.permutation(first, tickets).astype(jnp.int32)
        chosen = jax.random.randint(second, (), 0, N_WIDE, dtype=jnp.int32)
        owners = jnp.arange(tickets, dtype=jnp.int32) // CAP
        score = jnp.where(owners == chosen, score - tickets, score)
        order = jnp.argsort(score, stable=True)[:HMAX]
        picked = owners[order]
        picked = picked[jax.random.permutation(third, HMAX)]
        local = jax.random.randint(fourth, (HMAX,), 0, ITEM_GRP, dtype=jnp.int32)
        return (picked * ITEM_GRP + local).astype(jnp.int32)
    return jax.vmap(one_user)(jax.random.split(key, N_WIDE))


def levels(key, dims, cuts, smallest, high):
    def one(dim, blocks):
        steps = jax.random.uniform(jax.random.fold_in(jax.random.fold_in(key, 6), dim), (blocks,), jnp.float32, smallest / len(cuts), high / len(cuts))
        return jnp.repeat(jnp.exp(steps), dims[dim] // blocks).reshape((-1,) + (1,) * (len(dims) - dim - 1))

    factor_of = one(*cuts[0])
    for cut in cuts[1:]:
        factor_of = factor_of * one(*cut)
    return factor_of


def split_up(count, total, bound, skew):
    portions = [(1 << 20) // math.isqrt(standing ** skew) + 1 for standing in range(2, count + 1)]
    surplus, given = total - bound - (count - 1), [1] * (count - 1)
    while surplus > 0:
        free = [i for i in range(count - 1) if given[i] < bound]
        whole, left = sum([portions[i] for i in free]), surplus
        for i in free:
            more = min(bound - given[i], max(1, left * portions[i] // whole), surplus)
            given[i] = given[i] + more
            surplus = surplus - more
    return np.array([bound] + given)


def ragged_sizes(stream_key, count, total, reach, slope):
    if count == 2:
        one = jax.random.randint(stream_key, (), max(1, total - reach), min(reach, total - 1) + 1)
        return jnp.stack([one, total - one])
    lengths = jnp.asarray(split_up(count, total, reach, slope), jnp.int32)
    couples = (count - 1) // 2
    giver, taker = lengths[1:1 + 2 * couples:2], lengths[2:2 + 2 * couples:2]
    slack = jnp.minimum(giver - 1, reach - taker)
    shifted = jax.random.randint(jax.random.fold_in(stream_key, 1), (couples,), 0, 1 << 20) % (slack + 1)
    lengths = lengths.at[1:1 + 2 * couples:2].set(giver - shifted).at[2:2 + 2 * couples:2].set(taker + shifted)
    return lengths[jax.random.permutation(jax.random.fold_in(stream_key, 2), count)]


def scatter_about(key, dims, scale, limit, pieces=(), kind=jnp.bfloat16):
    values = scale * jax.random.normal(key, dims, jnp.float32)
    if pieces:
        values = values * levels(key, dims, pieces, -0.22, 0.18)
    return jnp.clip(values, -limit, limit).astype(kind)


def setup_inputs(seed: int = 0) -> dict:
    key_list = jax.random.split(jax.random.key(seed), 12)
    item_states = draw_item_states(jax.random.fold_in(key_list[11], 71), 0)
    item_gain = jnp.clip(1.0 + 0.1 * jax.random.normal(key_list[1], (D,), jnp.float32), 0.5, 1.5).astype(jnp.bfloat16)
    wq_item = draw_wq_item(jax.random.fold_in(key_list[11], 71), 0)
    wkv_item = draw_wkv_item(jax.random.fold_in(key_list[11], 71), 0)
    wo_item = scatter_about(key_list[4], (HEADS * HEAD_DIM, D), (HEADS * HEAD_DIM) ** -0.5, 0.125, ((0, 8),))
    user_gain = jnp.clip(1.0 + 0.1 * jax.random.normal(key_list[5], (D,), jnp.float32), 0.5, 1.5).astype(jnp.bfloat16)
    wq_user = draw_wq_user(jax.random.fold_in(key_list[11], 71), 0)
    wkv_user = draw_wkv_user(jax.random.fold_in(key_list[11], 71), 0)
    wo_user = scatter_about(key_list[8], (HEADS * HEAD_DIM, D), (HEADS * HEAD_DIM) ** -0.5, 0.125, ((0, 8), (1, 64)))
    history_items = draw_history_items(jax.random.fold_in(key_list[11], 71), 0)
    history_lengths = ragged_sizes(key_list[10], N_WIDE, N_WIDE * HMAX // 2, HMAX, 2).astype(jnp.int32)
    return {"item_states": item_states, "item_gain": item_gain, "wq_item": wq_item, "wkv_item": wkv_item, "wo_item": wo_item, "user_gain": user_gain, "wq_user": wq_user, "wkv_user": wkv_user, "wo_user": wo_user, "history_items": history_items, "history_lengths": history_lengths}


epsilon = 1e-05

def rms_scale(values, gain):
    wide = values.astype(jnp.float32)
    power = lax.optimization_barrier(jnp.mean(wide * wide, axis=-1, keepdims=True))
    return (wide * lax.rsqrt(power + epsilon) * gain.astype(jnp.float32)).astype(jnp.bfloat16)

def reference(item_states, item_gain, wq_item, wkv_item, wo_item, user_gain, wq_user, wkv_user, wo_user, history_items, history_lengths):
    per_item = item_states.reshape(ITEMS, TXT, D)
    scale = 1.0 / math.sqrt(HEAD_DIM)

    def encode(states):
        normed = rms_scale(states, item_gain)
        keyvals = jnp.dot(normed, wkv_item.reshape(D, -1), preferred_element_type=jnp.float32).astype(jnp.bfloat16)
        keyvals = keyvals.reshape(TXT, KV_HEADS, 2 * HEAD_DIM)
        query = jnp.dot(normed[-1:], wq_item, preferred_element_type=jnp.float32).astype(jnp.bfloat16)
        query = query.reshape(KV_HEADS, HEADS // KV_HEADS, HEAD_DIM)
        scores = jnp.einsum('krd,tkd->krt', query.astype(jnp.float32), keyvals[..., :HEAD_DIM].astype(jnp.float32)) * scale
        weights = jax.nn.softmax(scores, axis=-1).astype(jnp.bfloat16)
        mixed = jnp.einsum('krt,tkd->krd', weights.astype(jnp.float32), keyvals[..., HEAD_DIM:].astype(jnp.float32))
        mixed = mixed.astype(jnp.bfloat16).reshape(1, HEADS * HEAD_DIM)
        projected = jnp.dot(mixed, wo_item, preferred_element_type=jnp.float32)
        return (states[-1:].astype(jnp.float32) + projected).astype(jnp.bfloat16)[0]
    item_embeddings = lax.map(encode, per_item)

    def user_layer(inputs):
        ids, length = inputs
        features = jnp.take(item_embeddings, ids, axis=0)
        normed = rms_scale(features, user_gain)
        queries = jnp.dot(normed, wq_user, preferred_element_type=jnp.float32).astype(jnp.bfloat16)
        queries = queries.reshape(HMAX, KV_HEADS, HEADS // KV_HEADS, HEAD_DIM)
        keyvals = jnp.dot(normed, wkv_user.reshape(D, -1), preferred_element_type=jnp.float32).astype(jnp.bfloat16)
        keyvals = keyvals.reshape(HMAX, KV_HEADS, 2 * HEAD_DIM)
        scores = jnp.einsum('ikrd,jkd->krij', queries.astype(jnp.float32), keyvals[..., :HEAD_DIM].astype(jnp.float32)) * scale
        slots = jnp.arange(HMAX, dtype=jnp.int32)
        allowed = (slots[None, :] <= slots[:, None]) & (slots[None, :] < length)
        scores = jnp.where(allowed[None, None], scores, -1e+30)
        weights = jax.nn.softmax(scores, axis=-1).astype(jnp.bfloat16)
        mixed = jnp.einsum('krij,jkd->ikrd', weights.astype(jnp.float32), keyvals[..., HEAD_DIM:].astype(jnp.float32))
        mixed = mixed.astype(jnp.bfloat16).reshape(HMAX, HEADS * HEAD_DIM)
        projected = jnp.dot(mixed, wo_user, preferred_element_type=jnp.float32)
        live = (slots < length)[:, None]
        return jnp.where(live, features.astype(jnp.float32) + projected, 0.0).astype(jnp.bfloat16)
    user_states = lax.map(user_layer, (history_items, history_lengths)).reshape(ROWS, D)
    return (item_embeddings, user_states)
```

```python
import math

import jax
import jax.numpy as jnp
from jax import lax
from jax.sharding import PartitionSpec as P

HEAD_DIM = 64
TXT = 128
epsilon = 1e-05


def rms_scale(values, gain):
    wide = values.astype(jnp.float32)
    power = jnp.mean(wide * wide, axis=-1, keepdims=True)
    return (wide * lax.rsqrt(power + epsilon) * gain.astype(jnp.float32)).astype(jnp.bfloat16)


def dot_t(left, right):
    return lax.dot_general(
        left, right, (((1,), (1,)), ((), ())), preferred_element_type=jnp.float32
    )


def spread(values, axis, groups=None):
    size = lax.axis_size(axis) if groups is None else len(groups[0])
    copies = jnp.broadcast_to(values[None], (size,) + values.shape)
    return lax.all_to_all(copies, axis, 0, 0, axis_index_groups=groups)


def local(
    item_states,
    item_gain,
    wq_item,
    wkv_item,
    wo_item,
    user_gain,
    wq_user,
    wkv_user,
    wo_user,
    history_items,
    history_lengths,
):
    width = item_states.shape[1]
    n_narrow = lax.axis_size("narrow")
    n_x = n_narrow // 2
    share = width // n_narrow
    me = lax.axis_index("narrow")
    core = me % 2
    same_core = [[2 * x + c for x in range(n_x)] for c in range(2)]
    scale = 1.0 / math.sqrt(HEAD_DIM)

    parts = jnp.concatenate(
        [wq_user, wkv_user.reshape(wkv_user.shape[0], -1), wo_user.T], axis=1
    )
    weights_all = lax.all_gather(parts, "wide", axis=0, tiled=True)

    last_raw = spread(item_states[TXT - 1 :], "narrow").reshape(n_narrow, width)
    last_normed = rms_scale(last_raw, item_gain)
    queries = jnp.dot(last_normed, wq_item, preferred_element_type=jnp.float32)
    queries = queries.astype(jnp.bfloat16)
    per = queries.shape[1] // HEAD_DIM
    wk = wkv_item[:, 0, :HEAD_DIM]
    wv = wkv_item[:, 0, HEAD_DIM:]
    probes = dot_t(queries.reshape(-1, HEAD_DIM), wk).astype(jnp.bfloat16)
    probes = lax.all_to_all(probes.reshape(n_narrow, per, width), "narrow", 0, 0)
    normed = rms_scale(item_states, item_gain)
    scores = dot_t(probes.reshape(-1, width), normed) * scale
    attn = jax.nn.softmax(scores, axis=-1).astype(jnp.bfloat16)
    pooled = jnp.dot(attn, normed, preferred_element_type=jnp.float32).astype(jnp.bfloat16)
    pooled = lax.all_to_all(pooled.reshape(n_narrow, per, width), "narrow", 0, 0)
    mixed = jnp.dot(pooled.reshape(-1, width), wv, preferred_element_type=jnp.float32)
    mixed = mixed.astype(jnp.bfloat16).reshape(n_narrow, -1)
    partial_sum = jnp.dot(mixed, wo_item, preferred_element_type=jnp.float32)
    pieces = partial_sum.reshape(n_narrow, n_narrow, share).transpose(1, 0, 2)
    total = jnp.sum(lax.all_to_all(pieces, "narrow", 0, 0), axis=0)
    last_share = lax.dynamic_slice_in_dim(last_raw, me * share, share, 1)
    item_part = (last_share.astype(jnp.float32) + total).astype(jnp.bfloat16)

    catalog_part = spread(item_part, "wide").reshape(-1, share)
    mine = spread(catalog_part, "narrow", same_core)
    other = lax.ppermute(mine, "narrow", [(i, i ^ 1) for i in range(n_narrow)])
    low = jnp.where(core == 0, mine, other)
    high = jnp.where(core == 0, other, mine)
    catalog = jnp.stack([low, high], axis=1).transpose(2, 0, 1, 3).reshape(-1, width)
    user_normed = rms_scale(catalog, user_gain)

    q_width = wq_user.shape[1]
    kv_width = 2 * HEAD_DIM
    projected = jnp.dot(
        user_normed, weights_all[:, : q_width + kv_width], preferred_element_type=jnp.float32
    ).astype(jnp.bfloat16)
    item_ids = history_items[0]
    slots = item_ids.shape[0]
    picks = (item_ids[:, None] == jnp.arange(catalog.shape[0], dtype=jnp.int32)[None, :]).astype(
        jnp.bfloat16
    )
    rows = jnp.dot(
        picks,
        jnp.concatenate([projected, catalog_part], axis=1),
        preferred_element_type=jnp.float32,
    ).astype(jnp.bfloat16)
    heads = q_width // HEAD_DIM
    user_queries = rows[:, :q_width].reshape(slots, heads, HEAD_DIM)
    keys = rows[:, q_width : q_width + HEAD_DIM]
    values = rows[:, q_width + HEAD_DIM : q_width + kv_width]
    residual = rows[:, q_width + kv_width :]
    length = history_lengths[0]
    user_scores = jnp.einsum(
        "ird,jd->rij", user_queries, keys, preferred_element_type=jnp.float32
    ) * scale
    index = jnp.arange(slots, dtype=jnp.int32)
    allowed = (index[None, :] <= index[:, None]) & (index[None, :] < length)
    user_scores = jnp.where(allowed[None], user_scores, -1e30)
    user_attn = jax.nn.softmax(user_scores, axis=-1).astype(jnp.bfloat16)
    user_mixed = jnp.einsum(
        "rij,jd->ird", user_attn, values, preferred_element_type=jnp.float32
    ).astype(jnp.bfloat16).reshape(slots, -1)

    wo_t = weights_all[:, q_width + kv_width :].reshape(n_x, 2, share, -1)
    wo_mine = lax.dynamic_index_in_dim(wo_t, core, 1, keepdims=False)
    wo_other = lax.dynamic_index_in_dim(wo_t, 1 - core, 1, keepdims=False)

    def project(weights):
        return jnp.einsum("ih,xch->xic", user_mixed, weights, preferred_element_type=jnp.float32)

    theirs = lax.ppermute(
        project(wo_other).astype(jnp.bfloat16), "narrow", [(i, i ^ 1) for i in range(n_narrow)]
    )
    pair = (project(wo_mine) + theirs.astype(jnp.float32)).astype(jnp.bfloat16)
    shares = lax.all_to_all(pair, "narrow", 0, 0, axis_index_groups=same_core)
    summed = jnp.sum(shares.astype(jnp.float32), axis=0)
    live = (index < length)[:, None]
    user_states = jnp.where(live, residual.astype(jnp.float32) + summed, 0.0).astype(jnp.bfloat16)
    return (item_part, user_states)


def solution(mesh):
    return jax.shard_map(
        local,
        mesh=mesh,
        in_specs=(
            P(("wide", "narrow"), None),
            P(),
            P(None, "narrow"),
            P(None, "narrow", None),
            P("narrow", None),
            P(),
            P("wide", "narrow"),
            P("wide", "narrow", None),
            P("narrow", "wide"),
            P("wide", None),
            P("wide"),
        ),
        out_specs=(P("wide", "narrow"), P("wide", "narrow")),
        check_vma=False,
    )
```

```python
import math

import jax
import jax.numpy as jnp
from jax import lax
from jax.sharding import PartitionSpec as P

HEAD_DIM = 64
TXT = 128
epsilon = 1e-05


def rms_scale(values, gain):
    wide = values.astype(jnp.float32)
    power = jnp.mean(wide * wide, axis=-1, keepdims=True)
    return (wide * lax.rsqrt(power + epsilon) * gain.astype(jnp.float32)).astype(jnp.bfloat16)


def dot_t(left, right):
    return lax.dot_general(
        left, right, (((1,), (1,)), ((), ())), preferred_element_type=jnp.float32
    )


def spread(values, axis, groups=None):
    size = lax.axis_size(axis) if groups is None else len(groups[0])
    copies = jnp.broadcast_to(values[None], (size,) + values.shape)
    return lax.all_to_all(copies, axis, 0, 0, axis_index_groups=groups)


def local(
    item_states,
    item_gain,
    wq_item,
    wkv_item,
    wo_item,
    user_gain,
    wq_user,
    wkv_user,
    wo_user,
    history_items,
    history_lengths,
):
    width = item_states.shape[1]
    n_narrow = lax.axis_size("narrow")
    n_x = n_narrow // 2
    share = width // n_narrow
    me = lax.axis_index("narrow")
    core = me % 2
    same_core = [[2 * x + c for x in range(n_x)] for c in range(2)]
    scale = 1.0 / math.sqrt(HEAD_DIM)

    wo_all = lax.all_gather(wo_user.T, "wide", axis=0, tiled=True)
    size = math.isqrt(lax.axis_size("wide"))
    same_y = [[y * size + z for z in range(size)] for y in range(size)]
    same_z = [[y * size + z for y in range(size)] for z in range(size)]
    depth = wq_user.shape[0]
    wq_all = spread(wq_user, "wide", same_y).reshape(-1, wq_user.shape[1])
    wq_all = spread(wq_all, "wide", same_z).reshape(width, -1)
    wkv_all = spread(wkv_user.reshape(depth, -1), "wide", same_z).reshape(size * depth, -1)
    wkv_all = spread(wkv_all, "wide", same_y).reshape(width, -1)

    last_raw = spread(item_states[TXT - 1 :], "narrow").reshape(n_narrow, width)
    last_normed = rms_scale(last_raw, item_gain)
    queries = jnp.dot(last_normed, wq_item, preferred_element_type=jnp.float32)
    queries = queries.astype(jnp.bfloat16)
    per = queries.shape[1] // HEAD_DIM
    wk = wkv_item[:, 0, :HEAD_DIM]
    wv = wkv_item[:, 0, HEAD_DIM:]
    probes = dot_t(queries.reshape(-1, HEAD_DIM), wk).astype(jnp.bfloat16)
    probes = lax.all_to_all(probes.reshape(n_narrow, per, width), "narrow", 0, 0)
    normed = rms_scale(item_states, item_gain)
    scores = dot_t(probes.reshape(-1, width), normed) * scale
    attn = jax.nn.softmax(scores, axis=-1).astype(jnp.bfloat16)
    pooled = jnp.dot(attn, normed, preferred_element_type=jnp.float32).astype(jnp.bfloat16)
    pooled = lax.all_to_all(pooled.reshape(n_narrow, per, width), "narrow", 0, 0)
    mixed = jnp.dot(pooled.reshape(-1, width), wv, preferred_element_type=jnp.float32)
    mixed = mixed.astype(jnp.bfloat16).reshape(n_narrow, -1)
    partial_sum = jnp.dot(mixed, wo_item, preferred_element_type=jnp.float32)
    total = jnp.sum(spread(partial_sum.astype(jnp.bfloat16), "narrow").astype(jnp.float32), axis=0)
    embedded = (last_raw.astype(jnp.float32) + total).astype(jnp.bfloat16)
    item_part = lax.dynamic_slice_in_dim(embedded, me * share, share, 1)
    user_normed = rms_scale(embedded, user_gain)
    turned = user_normed.reshape(-1, size, size, depth).swapaxes(1, 2).reshape(-1, width)

    q_width = wq_user.shape[1]
    kv_width = 2 * HEAD_DIM
    projected = jnp.concatenate(
        [
            jnp.dot(user_normed, wq_all, preferred_element_type=jnp.float32),
            jnp.dot(turned, wkv_all, preferred_element_type=jnp.float32),
        ],
        axis=1,
    ).astype(jnp.bfloat16)
    group = projected.shape[0]
    catalog = spread(projected, "wide", same_y).reshape(size * group, -1)
    catalog = spread(catalog, "wide", same_z).reshape(size * size * group, -1)
    features = spread(item_part, "wide", same_z).reshape(size * group, -1)
    features = spread(features, "wide", same_y).reshape(size * size * group, -1)

    item_ids = history_items[0]
    slots = item_ids.shape[0]
    every = jnp.arange(catalog.shape[0], dtype=jnp.int32)[None, :]
    picks = (item_ids[:, None] == every).astype(jnp.bfloat16)
    rows = jnp.dot(picks, catalog, preferred_element_type=jnp.float32).astype(jnp.bfloat16)
    y_of = item_ids // (size * group)
    z_of = item_ids // group % size
    turned_ids = (z_of * size + y_of) * group + item_ids % group
    turned_picks = (turned_ids[:, None] == every).astype(jnp.bfloat16)
    residual = jnp.dot(turned_picks, features, preferred_element_type=jnp.float32)
    heads = q_width // HEAD_DIM
    user_queries = rows[:, :q_width].reshape(slots, heads, HEAD_DIM)
    keys = rows[:, q_width : q_width + HEAD_DIM]
    values = rows[:, q_width + HEAD_DIM :]
    length = history_lengths[0]
    user_scores = jnp.einsum(
        "ird,jd->rij", user_queries, keys, preferred_element_type=jnp.float32
    ) * scale
    index = jnp.arange(slots, dtype=jnp.int32)
    allowed = (index[None, :] <= index[:, None]) & (index[None, :] < length)
    user_scores = jnp.where(allowed[None], user_scores, -1e30)
    user_attn = jax.nn.softmax(user_scores, axis=-1).astype(jnp.bfloat16)
    user_mixed = jnp.einsum(
        "rij,jd->ird", user_attn, values, preferred_element_type=jnp.float32
    ).astype(jnp.bfloat16).reshape(slots, -1)

    wo_t = wo_all.reshape(n_x, 2, share, -1)
    wo_mine = lax.dynamic_index_in_dim(wo_t, core, 1, keepdims=False)
    wo_other = lax.dynamic_index_in_dim(wo_t, 1 - core, 1, keepdims=False)

    def project(weights):
        return jnp.einsum("ih,xch->xic", user_mixed, weights, preferred_element_type=jnp.float32)

    theirs = lax.ppermute(
        project(wo_other).astype(jnp.bfloat16), "narrow", [(i, i ^ 1) for i in range(n_narrow)]
    )
    pair = (project(wo_mine) + theirs.astype(jnp.float32)).astype(jnp.bfloat16)
    shares = lax.all_to_all(pair, "narrow", 0, 0, axis_index_groups=same_core)
    summed = jnp.sum(shares.astype(jnp.float32), axis=0)
    live = (index < length)[:, None]
    user_states = jnp.where(live, residual + summed, 0.0).astype(jnp.bfloat16)
    return (item_part, user_states)


def solution(mesh):
    return jax.shard_map(
        local,
        mesh=mesh,
        in_specs=(
            P(("wide", "narrow"), None),
            P(),
            P(None, "narrow"),
            P(None, "narrow", None),
            P("narrow", None),
            P(),
            P("wide", "narrow"),
            P("wide", "narrow", None),
            P("narrow", "wide"),
            P("wide", None),
            P("wide"),
        ),
        out_specs=(P("wide", "narrow"), P("wide", "narrow")),
        check_vma=False,
    )
```

```python
import math

import jax
import jax.numpy as jnp
from jax import lax
from jax.experimental import pallas as pl
from jax.experimental.pallas import tpu as pltpu
from jax.sharding import Mesh
from jax.sharding import PartitionSpec as P

HEAD_DIM = 64
TXT = 128
epsilon = 1e-05
VMEM_LIMIT = 40 * 1024 * 1024
WIDE = ("yh", "yl", "z")
NARROW = ("x", "core")


def rms_scale(values, gain):
    wide = values.astype(jnp.float32)
    power = jnp.mean(wide * wide, axis=-1, keepdims=True)
    return (wide * lax.rsqrt(power + epsilon) * gain.astype(jnp.float32)).astype(jnp.bfloat16)


def dot_t(left, right):
    return lax.dot_general(
        left, right, (((1,), (1,)), ((), ())), preferred_element_type=jnp.float32
    )


def spread(values, axis):
    copies = jnp.broadcast_to(values[None], (lax.axis_size(axis),) + values.shape)
    return lax.all_to_all(copies, axis, 0, 0)


def swap_cores(values):
    return lax.ppermute(values, "core", [(0, 1), (1, 0)])


def norm_kernel(core_ref, mine_ref, other_ref, gain_ref, out_ref):
    core = core_ref[0]
    pairs, n_x, rows, share = mine_ref.shape
    width = 2 * n_x * share
    for p in range(pairs):
        power = jnp.zeros((rows, share), jnp.float32)
        for x in range(n_x):
            for ref in (mine_ref, other_ref):
                block = ref[p, x].astype(jnp.float32)
                power = power + block * block
        factor = lax.rsqrt(jnp.sum(power, axis=1, keepdims=True) / width + epsilon)
        for x in range(n_x):
            for ref, where in ((mine_ref, 2 * x + core), (other_ref, 2 * x + 1 - core)):
                columns = pl.ds(pl.multiple_of(where * share, share), share)
                gain = gain_ref[:, columns].astype(jnp.float32)
                block = ref[p, x].astype(jnp.float32) * factor * gain
                out_ref[p * rows : (p + 1) * rows, columns] = block.astype(jnp.bfloat16)


def user_kernel(scalar_ref, normed_ref, weights_ref, places_ref, mixed_ref, terms_ref, picked_ref):
    length, core = scalar_ref[0], scalar_ref[1]
    slots, q_width = mixed_ref.shape
    share = terms_ref.shape[2]
    kv_at = q_width + 2 * HEAD_DIM
    projected = jnp.dot(
        normed_ref[...], weights_ref[:, :kv_at], preferred_element_type=jnp.float32
    ).astype(jnp.bfloat16)
    catalog = normed_ref.shape[0]
    every = lax.broadcasted_iota(jnp.int32, (slots, catalog), 1)
    picks = jnp.where(places_ref[...] == every, 1.0, 0.0).astype(jnp.bfloat16)
    picked_ref[...] = jnp.dot(picks, projected, preferred_element_type=jnp.float32).astype(
        jnp.bfloat16
    )
    scale = 1.0 / math.sqrt(HEAD_DIM)
    chunk = min(slots, 256)
    for start in range(0, slots, chunk):
        upto = start + chunk
        keys = picked_ref[:upto, q_width : q_width + HEAD_DIM]
        values = picked_ref[:upto, q_width + HEAD_DIM : kv_at]
        row = start + lax.broadcasted_iota(jnp.int32, (chunk, upto), 0)
        column = lax.broadcasted_iota(jnp.int32, (chunk, upto), 1)
        allowed = (column <= row) & (column < length)
        for head in range(q_width // HEAD_DIM):
            lanes = slice(head * HEAD_DIM, (head + 1) * HEAD_DIM)
            scores = dot_t(picked_ref[start:upto, lanes], keys) * scale
            scores = jnp.where(allowed, scores, -1e30)
            top = jnp.max(scores, axis=1, keepdims=True)
            parts = jnp.exp(scores - top)
            total = jnp.sum(parts, axis=1, keepdims=True)
            mixed = jnp.dot(parts.astype(jnp.bfloat16), values, preferred_element_type=jnp.float32)
            mixed_ref[start:upto, lanes] = (mixed / total).astype(jnp.bfloat16)
    for x in range(terms_ref.shape[0]):
        rows = pl.ds(pl.multiple_of((2 * x + 1 - core) * share, share), share)
        terms = dot_t(mixed_ref[...], weights_ref[rows, kv_at:])
        terms_ref[x] = terms.astype(jnp.bfloat16)


def pair_kernel(core_ref, mixed_ref, weights_ref, theirs_ref, pair_ref):
    core = core_ref[0]
    share = pair_ref.shape[2]
    for x in range(pair_ref.shape[0]):
        rows = pl.ds(pl.multiple_of((2 * x + core) * share, share), share)
        terms = dot_t(mixed_ref[...], weights_ref[rows, -mixed_ref.shape[1] :])
        pair_ref[x] = (terms + theirs_ref[x].astype(jnp.float32)).astype(jnp.bfloat16)


SMEM = pl.BlockSpec(memory_space=pltpu.SMEM)
VMEM = pl.BlockSpec(memory_space=pltpu.VMEM)


def call(kernel, name, outs, ins, scratch=()):
    return pl.pallas_call(
        kernel,
        name=name,
        out_shape=outs,
        in_specs=[SMEM] + [VMEM] * (len(ins) - 1),
        out_specs=jax.tree.map(lambda _: VMEM, outs),
        scratch_shapes=scratch,
        compiler_params=pltpu.CompilerParams(vmem_limit_bytes=VMEM_LIMIT),
    )(*ins)


def local(
    item_states,
    item_gain,
    wq_item,
    wkv_item,
    wo_item,
    user_gain,
    wq_user,
    wkv_user,
    wo_user,
    history_items,
    history_lengths,
):
    width = item_states.shape[1]
    n_x = lax.axis_size("x")
    n_narrow = 2 * n_x
    share = width // n_narrow
    core = lax.axis_index("core")
    me = lax.axis_index("x") * 2 + core
    scale = 1.0 / math.sqrt(HEAD_DIM)

    parts = jnp.concatenate(
        [wq_user, wkv_user.reshape(wkv_user.shape[0], -1), wo_user.T], axis=1
    )
    parts, last_row = lax.optimization_barrier((parts, item_states[TXT - 1 :]))
    weights_all = lax.all_gather(parts, WIDE, axis=0, tiled=True)

    last_raw = spread(last_row, NARROW).reshape(n_narrow, width)
    last_normed = rms_scale(last_raw, item_gain)
    queries = jnp.dot(last_normed, wq_item, preferred_element_type=jnp.float32)
    queries = queries.astype(jnp.bfloat16)
    per = queries.shape[1] // HEAD_DIM
    wk = wkv_item[:, 0, :HEAD_DIM]
    wv = wkv_item[:, 0, HEAD_DIM:]
    probes = dot_t(queries.reshape(-1, HEAD_DIM), wk).astype(jnp.bfloat16)
    probes = lax.all_to_all(probes.reshape(n_narrow, per, width), NARROW, 0, 0)
    normed = rms_scale(item_states, item_gain)
    scores = dot_t(probes.reshape(-1, width), normed) * scale
    attn = jax.nn.softmax(scores, axis=-1).astype(jnp.bfloat16)
    pooled = jnp.dot(attn, normed, preferred_element_type=jnp.float32).astype(jnp.bfloat16)
    pooled = lax.all_to_all(pooled.reshape(n_narrow, per, width), NARROW, 0, 0)
    mixed = jnp.dot(pooled.reshape(-1, width), wv, preferred_element_type=jnp.float32)
    mixed = mixed.astype(jnp.bfloat16).reshape(n_narrow, -1)
    partial_sum = jnp.dot(mixed, wo_item, preferred_element_type=jnp.float32)
    pieces = partial_sum.reshape(n_narrow, n_narrow, share).transpose(1, 0, 2)
    total = jnp.sum(lax.all_to_all(pieces, NARROW, 0, 0), axis=0)
    last_share = lax.dynamic_slice_in_dim(last_raw, me * share, share, 1)
    item_part = (last_share.astype(jnp.float32) + total).astype(jnp.bfloat16)

    n_z, n_pair, n_far = lax.axis_size("z"), lax.axis_size("yl"), lax.axis_size("yh")
    group = item_part.shape[0]
    block = spread(item_part, "z").reshape(n_z * group, share)
    block = spread(block, "yh").reshape(n_far * n_z * group, share)
    mine = spread(block, ("yl", "x")).reshape(n_pair, n_x, -1, share)
    other = swap_cores(mine)
    core_one = core[None].astype(jnp.int32)
    catalog = n_pair * mine.shape[2]
    user_normed = call(
        norm_kernel,
        "norm_catalog",
        jax.ShapeDtypeStruct((catalog, width), jnp.bfloat16),
        (core_one, mine, other, user_gain[None]),
    )

    item_ids = history_items[0]
    slots = item_ids.shape[0]
    length = history_lengths[0]
    of_y, in_y = item_ids // (n_z * group), item_ids % (n_z * group)
    places = ((of_y % n_pair) * n_far + of_y // n_pair) * (n_z * group) + in_y
    user_mixed, theirs = call(
        user_kernel,
        "user_attention",
        (
            jax.ShapeDtypeStruct((slots, wq_user.shape[1]), jnp.bfloat16),
            jax.ShapeDtypeStruct((n_x, slots, share), jnp.bfloat16),
        ),
        (
            jnp.stack([length, core]).astype(jnp.int32),
            user_normed,
            weights_all,
            places[:, None],
        ),
        [pltpu.VMEM((slots, wq_user.shape[1] + 2 * HEAD_DIM), jnp.bfloat16)],
    )

    theirs = swap_cores(theirs)
    pair = call(
        pair_kernel,
        "pair_sum",
        jax.ShapeDtypeStruct(theirs.shape, jnp.bfloat16),
        (core_one, user_mixed, weights_all, theirs),
    )
    shares = lax.all_to_all(pair, "x", 0, 0)
    own = lax.dynamic_index_in_dim(mine, lax.axis_index("x"), 1, keepdims=False)
    picks = (places[:, None] == jnp.arange(catalog, dtype=jnp.int32)[None, :]).astype(jnp.bfloat16)
    residual = jnp.dot(picks, own.reshape(-1, share), preferred_element_type=jnp.float32)
    summed = jnp.sum(shares.astype(jnp.float32), axis=0)
    live = (jnp.arange(slots, dtype=jnp.int32) < length)[:, None]
    user_states = jnp.where(live, residual + summed, 0.0).astype(jnp.bfloat16)
    return (item_part, user_states)


def solution(mesh):
    n_wide, n_narrow = mesh.shape["wide"], mesh.shape["narrow"]
    side = math.isqrt(n_wide)
    fine = Mesh(
        mesh.devices.reshape(side // 2, 2, n_wide // side, n_narrow // 2, 2), WIDE + NARROW
    )
    return jax.shard_map(
        local,
        mesh=fine,
        in_specs=(
            P(WIDE + NARROW, None),
            P(),
            P(None, NARROW),
            P(None, NARROW, None),
            P(NARROW, None),
            P(),
            P(WIDE, NARROW),
            P(WIDE, NARROW, None),
            P(NARROW, WIDE),
            P(WIDE, None),
            P(WIDE),
        ),
        out_specs=(P(WIDE, NARROW), P(WIDE, NARROW)),
        check_vma=False,
    )
```

```python
import math

import jax
import jax.numpy as jnp
from jax import lax
from jax.experimental import pallas as pl
from jax.experimental.pallas import tpu as pltpu
from jax.sharding import Mesh
from jax.sharding import PartitionSpec as P

HEAD_DIM = 64
TXT = 128
epsilon = 1e-05
MIB = 1024 * 1024
WIDE = ("y", "z")
NARROW = ("x", "core")


def rms_scale(values, gain):
    wide = values.astype(jnp.float32)
    power = jnp.mean(wide * wide, axis=-1, keepdims=True)
    return (wide * lax.rsqrt(power + epsilon) * gain.astype(jnp.float32)).astype(jnp.bfloat16)


def dot_t(left, right):
    return lax.dot_general(
        left, right, (((1,), (1,)), ((), ())), preferred_element_type=jnp.float32
    )


def spread(values, axis):
    copies = jnp.broadcast_to(values[None], (lax.axis_size(axis),) + values.shape)
    return lax.all_to_all(copies, axis, 0, 0)


def swap_cores(values):
    return lax.ppermute(values, "core", [(0, 1), (1, 0)])


def along_x(values, step):
    n_x = lax.axis_size("x")
    pairs = [
        (2 * x + core, 2 * ((x + step * (1 - 2 * core)) % n_x) + core)
        for x in range(n_x)
        for core in range(2)
    ]
    return lax.ppermute(values, NARROW, pairs)


def load(source, target, sem):
    copy = pltpu.make_async_copy(source, target, sem)
    copy.start()
    return copy


def first_kernel(wq_ref, wkv_ref, wo_ref, parts_ref, sems):
    at, loads = 0, []
    for k, ref in enumerate((wq_ref, wkv_ref, wo_ref)):
        columns = ref.shape[1]
        loads.append(load(ref, parts_ref.at[:, pl.ds(at, columns)], sems.at[k]))
        at += columns
    for copy in loads:
        copy.wait()


def message_kernel(parts_ref, states_ref, message_ref, tail_ref, sem):
    del parts_ref
    tail = tail_ref.shape[0]
    load(states_ref.at[pl.ds(TXT - tail, tail)], tail_ref, sem).wait()
    row = tail_ref[...].astype(jnp.float32)[-1:]
    pieces, share = message_ref.shape[1:]
    tile = jnp.concatenate([row[:, j * share : (j + 1) * share] for j in range(pieces)], axis=0)
    for k in range(message_ref.shape[0]):
        message_ref[k] = tile


def user_kernel(
    scalar_ref,
    gain_ref,
    places_ref,
    mine_ref,
    other_ref,
    weights_ref,
    mixed_ref,
    terms_ref,
    wo_ref,
    normed_ref,
    picked_ref,
):
    length, core, place = scalar_ref[0], scalar_ref[1], scalar_ref[2]
    slots, q_width = mixed_ref.shape
    n_x, share = wo_ref.shape[:2]
    blocks = 2 * n_x
    kv_at = weights_ref.shape[1] - q_width
    catalog = normed_ref.shape[1]
    raw = [ref[x] for x in range(n_x) for ref in (mine_ref, other_ref)]
    power = jnp.zeros((catalog, share), jnp.float32)
    for k in range(blocks):
        block = raw[k].astype(jnp.float32)
        power = power + block * block
    factor = lax.rsqrt(jnp.sum(power, axis=1, keepdims=True) / (blocks * share) + epsilon)
    for k in range(blocks):
        where = k + core if k % 2 == 0 else k - core
        columns = pl.ds(pl.multiple_of(where * share, share), share)
        gain = gain_ref[:, columns].astype(jnp.float32)
        normed_ref[where] = (raw[k].astype(jnp.float32) * factor * gain).astype(jnp.bfloat16)
    every = lax.broadcasted_iota(jnp.int32, (slots, catalog), 1)
    picks = jnp.where(places_ref[...] == every, 1.0, 0.0).astype(jnp.bfloat16)
    projected = jnp.zeros((catalog, kv_at), jnp.float32)
    for k in range(blocks):
        projected += jnp.dot(
            normed_ref[k],
            weights_ref[k * share : (k + 1) * share, :kv_at],
            preferred_element_type=jnp.float32,
        )
    picked_ref[...] = jnp.dot(
        picks, projected.astype(jnp.bfloat16), preferred_element_type=jnp.float32
    ).astype(jnp.bfloat16)
    scale = 1.0 / math.sqrt(HEAD_DIM)
    chunk = min(slots, 256)
    for start in range(0, slots, chunk):
        upto = start + chunk
        keys = picked_ref[:upto, q_width : q_width + HEAD_DIM]
        values = picked_ref[:upto, q_width + HEAD_DIM : kv_at]
        row = start + lax.broadcasted_iota(jnp.int32, (chunk, upto), 0)
        column = lax.broadcasted_iota(jnp.int32, (chunk, upto), 1)
        allowed = (column <= row) & (column < length)
        for head in range(q_width // HEAD_DIM):
            lanes = slice(head * HEAD_DIM, (head + 1) * HEAD_DIM)
            scores = dot_t(picked_ref[start:upto, lanes], keys) * scale
            scores = jnp.where(allowed, scores, -1e30)
            top = jnp.max(scores, axis=1, keepdims=True)
            parts = jnp.exp(scores - top)
            total = jnp.sum(parts, axis=1, keepdims=True)
            mixed = jnp.dot(parts.astype(jnp.bfloat16), values, preferred_element_type=jnp.float32)
            mixed_ref[start:upto, lanes] = (mixed / total).astype(jnp.bfloat16)
    step = 1 - 2 * core
    for k, (theirs, mine) in enumerate(((2, 2), (step, -step), (-step, step), (0, 0))):
        rows = (2 * lax.rem(place + n_x + theirs, n_x) + 1 - core) * share
        rows = pl.ds(pl.multiple_of(rows, share), share)
        terms_ref[k] = dot_t(mixed_ref[...], weights_ref[rows, kv_at:]).astype(jnp.bfloat16)
        rows = (2 * lax.rem(place + n_x + mine, n_x) + core) * share
        rows = pl.ds(pl.multiple_of(rows, share), share)
        wo_ref[k] = weights_ref[rows, kv_at:]


def pair_kernel(mixed_ref, wo_ref, theirs_ref, *pair_refs):
    for x, ref in enumerate(pair_refs):
        terms = dot_t(mixed_ref[...], wo_ref[x])
        ref[...] = (terms + theirs_ref[x].astype(jnp.float32)).astype(jnp.bfloat16)


SMEM = pl.BlockSpec(memory_space=pltpu.SMEM)
VMEM = pl.BlockSpec(memory_space=pltpu.VMEM)
ANY = pl.BlockSpec(memory_space=pl.ANY)


def call(kernel, name, limit, outs, in_specs, ins, scratch=()):
    return pl.pallas_call(
        kernel,
        name=name,
        out_shape=outs,
        in_specs=in_specs,
        out_specs=jax.tree.map(lambda _: VMEM, outs),
        scratch_shapes=scratch,
        compiler_params=pltpu.CompilerParams(vmem_limit_bytes=limit * MIB),
    )(*ins)


def local(
    item_states,
    item_gain,
    wq_item,
    wkv_item,
    wo_item,
    user_gain,
    wq_user,
    wkv_user,
    wo_user,
    history_items,
    history_lengths,
):
    width = item_states.shape[1]
    n_x = lax.axis_size("x")
    n_narrow = 2 * n_x
    share = width // n_narrow
    core = lax.axis_index("core")
    me = lax.axis_index("x") * 2 + core
    scale = 1.0 / math.sqrt(HEAD_DIM)

    columns = wq_user.shape[1] + 2 * HEAD_DIM + wo_user.shape[0]
    parts = call(
        first_kernel,
        "user_weights",
        60,
        jax.ShapeDtypeStruct((wq_user.shape[0], columns), jnp.bfloat16),
        [ANY] * 3,
        (wq_user, wkv_user.reshape(wkv_user.shape[0], -1), wo_user.T),
        [pltpu.SemaphoreType.DMA((3,))],
    )
    weights_all = lax.all_gather(parts, WIDE, axis=0, tiled=True)

    messages = call(
        message_kernel,
        "last_rows",
        60,
        jax.ShapeDtypeStruct((n_narrow, n_narrow, share), jnp.float32),
        [ANY, ANY],
        (parts, item_states),
        [pltpu.VMEM((16, width), jnp.bfloat16), pltpu.SemaphoreType.DMA],
    )
    last_raw = lax.all_to_all(messages, NARROW, 0, 0)
    last_share = lax.dynamic_index_in_dim(last_raw, me, 1, keepdims=False)
    last_raw = last_raw.reshape(n_narrow, width)
    last_normed = rms_scale(last_raw, item_gain)
    queries = jnp.dot(last_normed, wq_item, preferred_element_type=jnp.float32)
    queries = queries.astype(jnp.bfloat16)
    per = queries.shape[1] // HEAD_DIM
    wk = wkv_item[:, 0, :HEAD_DIM]
    wv = wkv_item[:, 0, HEAD_DIM:]
    probes = dot_t(queries.reshape(-1, HEAD_DIM), wk).astype(jnp.bfloat16)
    probes = lax.all_to_all(probes.reshape(n_narrow, per, width), NARROW, 0, 0)
    length = history_lengths[0]
    normed, places, scalars, gain_row = lax.optimization_barrier(
        (
            rms_scale(item_states, item_gain),
            history_items[0][:, None],
            jnp.stack([length, core, lax.axis_index("x")]).astype(jnp.int32),
            user_gain[None],
        )
    )
    scores = dot_t(probes.reshape(-1, width), normed) * scale
    attn = jax.nn.softmax(scores, axis=-1).astype(jnp.bfloat16)
    pooled = jnp.dot(attn, normed, preferred_element_type=jnp.float32).astype(jnp.bfloat16)
    pooled = lax.all_to_all(pooled.reshape(n_narrow, per, width), NARROW, 0, 0)
    mixed = jnp.dot(pooled.reshape(-1, width), wv, preferred_element_type=jnp.float32)
    mixed = mixed.astype(jnp.bfloat16).reshape(n_narrow, -1)
    partial_sum = jnp.dot(mixed, wo_item, preferred_element_type=jnp.float32)
    pieces = partial_sum.reshape(n_narrow, n_narrow, share).transpose(1, 0, 2)
    total = jnp.sum(lax.all_to_all(pieces, NARROW, 0, 0), axis=0)
    item_part = (last_share + total).astype(jnp.bfloat16)

    block = spread(item_part, WIDE).reshape(-1, share)
    mine = spread(block, "x")
    other = swap_cores(mine)
    catalog = block.shape[0]
    slots = history_items.shape[1]
    heads_width = wq_user.shape[1]
    kv_at = heads_width + 2 * HEAD_DIM
    user_mixed, theirs, wo_mine = call(
        user_kernel,
        "user_attention",
        20,
        (
            jax.ShapeDtypeStruct((slots, heads_width), jnp.bfloat16),
            jax.ShapeDtypeStruct((n_x, slots, share), jnp.bfloat16),
            jax.ShapeDtypeStruct((n_x, share, heads_width), jnp.bfloat16),
        ),
        [SMEM] + [VMEM] * 5,
        (
            scalars,
            gain_row,
            places,
            mine,
            other,
            weights_all,
        ),
        [
            pltpu.VMEM((n_narrow, catalog, share), jnp.bfloat16),
            pltpu.VMEM((slots, kv_at), jnp.bfloat16),
        ],
    )

    theirs = swap_cores(theirs)
    first, direct, second, own = call(
        pair_kernel,
        "pair_sum",
        20,
        [jax.ShapeDtypeStruct((slots, share), jnp.bfloat16)] * n_x,
        [VMEM] * 3,
        (user_mixed, wo_mine, theirs),
    )
    relay = along_x(first, 1)
    direct = along_x(direct, -1)
    relay = (relay.astype(jnp.float32) + second.astype(jnp.float32)).astype(jnp.bfloat16)
    relay = along_x(relay, 1)
    picks = (places == jnp.arange(catalog, dtype=jnp.int32)[None, :]).astype(jnp.bfloat16)
    residual = jnp.dot(picks, block, preferred_element_type=jnp.float32)
    summed = own.astype(jnp.float32) + direct.astype(jnp.float32) + relay.astype(jnp.float32)
    live = (jnp.arange(slots, dtype=jnp.int32) < length)[:, None]
    user_states = jnp.where(live, residual + summed, 0.0).astype(jnp.bfloat16)
    return (item_part, user_states)


def solution(mesh):
    n_wide, n_narrow = mesh.shape["wide"], mesh.shape["narrow"]
    side = math.isqrt(n_wide)
    fine = Mesh(
        mesh.devices.reshape(side, n_wide // side, n_narrow // 2, 2), WIDE + NARROW
    )
    return jax.shard_map(
        local,
        mesh=fine,
        in_specs=(
            P(WIDE + NARROW, None),
            P(),
            P(None, NARROW),
            P(None, NARROW, None),
            P(NARROW, None),
            P(),
            P(WIDE, NARROW),
            P(WIDE, NARROW, None),
            P(NARROW, WIDE),
            P(WIDE, None),
            P(WIDE),
        ),
        out_specs=(P(WIDE, NARROW), P(WIDE, NARROW)),
        check_vma=False,
    )
```

```python
import math

import jax
import jax.numpy as jnp
from jax import lax
from jax.experimental import pallas as pl
from jax.experimental.pallas import tpu as pltpu
from jax.sharding import Mesh
from jax.sharding import PartitionSpec as P

HEAD_DIM = 64
TXT = 128
epsilon = 1e-05
MIB = 1024 * 1024
WIDE = ("y", "z")
NARROW = ("x", "core")


def rms_scale(values, gain):
    wide = values.astype(jnp.float32)
    power = jnp.mean(wide * wide, axis=-1, keepdims=True)
    return (wide * lax.rsqrt(power + epsilon) * gain.astype(jnp.float32)).astype(jnp.bfloat16)


def dot_t(left, right):
    return lax.dot_general(
        left, right, (((1,), (1,)), ((), ())), preferred_element_type=jnp.float32
    )


def spread(values, axis):
    copies = jnp.broadcast_to(values[None], (lax.axis_size(axis),) + values.shape)
    return lax.all_to_all(copies, axis, 0, 0)


def swap_cores(values):
    return lax.ppermute(values, "core", [(0, 1), (1, 0)])


def along_x(values, step):
    n_x = lax.axis_size("x")
    pairs = [
        (2 * x + core, 2 * ((x + step * (1 - 2 * core)) % n_x) + core)
        for x in range(n_x)
        for core in range(2)
    ]
    return lax.ppermute(values, NARROW, pairs)


def load(source, target, sem):
    copy = pltpu.make_async_copy(source, target, sem)
    copy.start()
    return copy


def first_kernel(wq_ref, wkv_ref, wo_ref, copies_ref, sems):
    at, loads = 0, []
    for k, ref in enumerate((wq_ref, wkv_ref, wo_ref)):
        columns = ref.shape[1]
        loads.append(load(ref, copies_ref.at[0, :, pl.ds(at, columns)], sems.at[k]))
        at += columns
    for copy in loads:
        copy.wait()
    for k in range(1, copies_ref.shape[0]):
        copies_ref[k] = copies_ref[0]


def message_kernel(states_ref, message_ref, tail_ref, sem):
    tail = tail_ref.shape[0]
    load(states_ref.at[pl.ds(TXT - tail, tail)], tail_ref, sem).wait()
    row = tail_ref[...].astype(jnp.float32)[-1:]
    pieces, share = message_ref.shape[1:]
    tile = jnp.concatenate([row[:, j * share : (j + 1) * share] for j in range(pieces)], axis=0)
    for k in range(message_ref.shape[0]):
        message_ref[k] = tile


def probe_kernel(gain_ref, last_ref, wq_ref, wkv_ref, probes_ref, raw_ref):
    raw = jnp.concatenate([last_ref[:, j, :] for j in range(last_ref.shape[1])], axis=1)
    raw_ref[...] = raw
    power = jnp.mean(raw * raw, axis=-1, keepdims=True)
    normed = raw * lax.rsqrt(power + epsilon) * gain_ref[...].astype(jnp.float32)
    queries = jnp.dot(normed.astype(jnp.bfloat16), wq_ref[...], preferred_element_type=jnp.float32)
    queries = queries.astype(jnp.bfloat16)
    keys = wkv_ref[:, :HEAD_DIM]
    for head in range(probes_ref.shape[1]):
        lanes = slice(head * HEAD_DIM, (head + 1) * HEAD_DIM)
        probes_ref[:, head, :] = dot_t(queries[:, lanes], keys).astype(jnp.bfloat16)


def pool_kernel(probes_ref, normed_ref, pooled_ref):
    items, per = probes_ref.shape[:2]
    probes = jnp.concatenate([probes_ref[k].astype(jnp.float32) for k in range(items)], axis=0)
    scores = dot_t(probes.astype(jnp.bfloat16), normed_ref[...]) * (1.0 / math.sqrt(HEAD_DIM))
    parts = jnp.exp(scores - jnp.max(scores, axis=1, keepdims=True))
    parts = parts / jnp.sum(parts, axis=1, keepdims=True)
    pooled = jnp.dot(parts.astype(jnp.bfloat16), normed_ref[...], preferred_element_type=jnp.float32)
    for k in range(items):
        pooled_ref[k] = pooled[k * per : (k + 1) * per].astype(jnp.bfloat16)


def project_kernel(
    scalar_ref,
    gain_ref,
    terms_ref,
    last_ref,
    weights_ref,
    copies_ref,
    embedded_ref,
):
    total = last_ref[...]
    for k in range(terms_ref.shape[0]):
        total = total + terms_ref[k].astype(jnp.float32)
    embedded = total.astype(jnp.bfloat16)
    embedded_ref[...] = embedded
    wide = embedded.astype(jnp.float32)
    power = jnp.mean(wide * wide, axis=-1, keepdims=True)
    normed = wide * lax.rsqrt(power + epsilon) * gain_ref[...].astype(jnp.float32)
    projected = jnp.dot(
        normed.astype(jnp.bfloat16),
        weights_ref[...],
        preferred_element_type=jnp.float32,
    ).astype(jnp.bfloat16)
    kv_at = projected.shape[1]
    share = copies_ref.shape[2] - kv_at
    columns = pl.ds(pl.multiple_of((2 * scalar_ref[2] + scalar_ref[1]) * share, share), share)
    features = embedded_ref[:, columns]
    for k in range(copies_ref.shape[0]):
        copies_ref[k, :, :kv_at] = projected
        copies_ref[k, :, kv_at:] = features


def layout_kernel(scalar_ref, weights_ref, theirs_ref, mine_ref):
    n_x, share, out_width = mine_ref.shape
    core, place = scalar_ref[1], scalar_ref[2]
    step = 1 - 2 * core
    for k, (theirs, mine) in enumerate(((2, 2), (step, -step), (-step, step), (0, 0))):
        rows = (2 * lax.rem(place + n_x + theirs, n_x) + 1 - core) * share
        rows = pl.ds(pl.multiple_of(rows, share), share)
        theirs_ref[k] = weights_ref[rows, -out_width:]
        rows = (2 * lax.rem(place + n_x + mine, n_x) + core) * share
        rows = pl.ds(pl.multiple_of(rows, share), share)
        mine_ref[k] = weights_ref[rows, -out_width:]


def user_kernel(
    scalar_ref, places_ref, catalog_ref, wo_ref, mixed_ref, terms_ref, residual_ref, picked_ref
):
    length = scalar_ref[0]
    slots, q_width = mixed_ref.shape
    catalog, kv_at = catalog_ref.shape[0], q_width + 2 * HEAD_DIM
    every = lax.broadcasted_iota(jnp.int32, (slots, catalog), 1)
    picks = jnp.where(places_ref[...] == every, 1.0, 0.0).astype(jnp.bfloat16)
    picked = jnp.dot(picks, catalog_ref[...], preferred_element_type=jnp.float32)
    picked_ref[...] = picked[:, :kv_at].astype(jnp.bfloat16)
    residual_ref[...] = picked[:, kv_at:].astype(jnp.bfloat16)
    scale = 1.0 / math.sqrt(HEAD_DIM)
    chunk = min(slots, 256)
    for start in range(0, slots, chunk):
        upto = start + chunk
        keys = picked_ref[:upto, q_width : q_width + HEAD_DIM]
        values = picked_ref[:upto, q_width + HEAD_DIM : kv_at]
        row = start + lax.broadcasted_iota(jnp.int32, (chunk, upto), 0)
        column = lax.broadcasted_iota(jnp.int32, (chunk, upto), 1)
        allowed = (column <= row) & (column < length)
        for head in range(q_width // HEAD_DIM):
            lanes = slice(head * HEAD_DIM, (head + 1) * HEAD_DIM)
            scores = dot_t(picked_ref[start:upto, lanes], keys) * scale
            scores = jnp.where(allowed, scores, -1e30)
            top = jnp.max(scores, axis=1, keepdims=True)
            parts = jnp.exp(scores - top)
            total = jnp.sum(parts, axis=1, keepdims=True)
            mixed = jnp.dot(parts.astype(jnp.bfloat16), values, preferred_element_type=jnp.float32)
            mixed_ref[start:upto, lanes] = (mixed / total).astype(jnp.bfloat16)
    for k in range(terms_ref.shape[0]):
        terms_ref[k] = dot_t(mixed_ref[...], wo_ref[k]).astype(jnp.bfloat16)


def pair_kernel(mixed_ref, wo_ref, theirs_ref, *pair_refs):
    for x, ref in enumerate(pair_refs):
        terms = dot_t(mixed_ref[...], wo_ref[x])
        ref[...] = (terms + theirs_ref[x].astype(jnp.float32)).astype(jnp.bfloat16)


SMEM = pl.BlockSpec(memory_space=pltpu.SMEM)
VMEM = pl.BlockSpec(memory_space=pltpu.VMEM)
ANY = pl.BlockSpec(memory_space=pl.ANY)


def call(kernel, name, limit, outs, in_specs, ins, scratch=()):
    return pl.pallas_call(
        kernel,
        name=name,
        out_shape=outs,
        in_specs=in_specs,
        out_specs=jax.tree.map(lambda _: VMEM, outs),
        scratch_shapes=scratch,
        compiler_params=pltpu.CompilerParams(vmem_limit_bytes=limit * MIB),
    )(*ins)


def local(
    item_states,
    item_gain,
    wq_item,
    wkv_item,
    wo_item,
    user_gain,
    wq_user,
    wkv_user,
    wo_user,
    history_items,
    history_lengths,
):
    width = item_states.shape[1]
    n_x = lax.axis_size("x")
    n_narrow = 2 * n_x
    share = width // n_narrow
    core = lax.axis_index("core")
    me = lax.axis_index("x") * 2 + core
    scale = 1.0 / math.sqrt(HEAD_DIM)

    columns = wq_user.shape[1] + 2 * HEAD_DIM + wo_user.shape[0]
    n_z = lax.axis_size("z")
    depth, heads_width = wq_user.shape
    kv_at = heads_width + 2 * HEAD_DIM
    columns = kv_at + wo_user.shape[0]
    copies = call(
        first_kernel,
        "user_weights",
        60,
        jax.ShapeDtypeStruct((n_z, depth, columns), jnp.bfloat16),
        [ANY] * 3,
        (wq_user, wkv_user.reshape(depth, -1), wo_user.T),
        [pltpu.SemaphoreType.DMA((3,))],
    )
    weights_z = lax.all_to_all(copies, "z", 0, 0).reshape(n_z * depth, columns)
    messages = call(
        message_kernel,
        "last_rows",
        20,
        jax.ShapeDtypeStruct((n_narrow, n_narrow, share), jnp.float32),
        [ANY],
        (item_states,),
        [pltpu.VMEM((16, width), jnp.bfloat16), pltpu.SemaphoreType.DMA],
    )
    length = history_lengths[0]
    weights_z, messages, normed, places, scalars, gain_row, item_gain_row = (
        lax.optimization_barrier(
            (
                weights_z,
                messages,
                rms_scale(item_states, item_gain),
                history_items[0][:, None],
                jnp.stack([length, core, lax.axis_index("x")]).astype(jnp.int32),
                user_gain[None],
                item_gain[None],
            )
        )
    )
    weights_all = lax.all_gather(weights_z, "y", axis=0, tiled=True)
    last_raw = lax.all_to_all(messages, NARROW, 0, 0)
    per = wq_item.shape[1] // HEAD_DIM
    wkv = wkv_item.reshape(width, -1)
    wv = wkv[:, HEAD_DIM:]
    probes, last_raw = call(
        probe_kernel,
        "item_probes",
        20,
        (
            jax.ShapeDtypeStruct((n_narrow, per, width), jnp.bfloat16),
            jax.ShapeDtypeStruct((n_narrow, width), jnp.float32),
        ),
        [VMEM] * 4,
        (item_gain_row, last_raw, wq_item, wkv),
    )
    probes = lax.all_to_all(probes, NARROW, 0, 0)
    pooled = call(
        pool_kernel,
        "item_attention",
        20,
        jax.ShapeDtypeStruct(probes.shape, jnp.bfloat16),
        [VMEM] * 2,
        (probes, normed),
    )
    pooled = lax.all_to_all(pooled, NARROW, 0, 0)
    mixed = jnp.dot(pooled.reshape(-1, width), wv, preferred_element_type=jnp.float32)
    mixed = mixed.astype(jnp.bfloat16).reshape(n_narrow, -1)
    partial_sum = jnp.dot(mixed, wo_item, preferred_element_type=jnp.float32)
    terms = spread(partial_sum.astype(jnp.bfloat16), NARROW)
    group = terms.shape[1]
    copies, embedded = call(
        project_kernel,
        "project_items",
        20,
        (
            jax.ShapeDtypeStruct((lax.axis_size(WIDE), group, kv_at + share), jnp.bfloat16),
            jax.ShapeDtypeStruct((group, width), jnp.bfloat16),
        ),
        [SMEM] + [VMEM] * 4,
        (scalars, gain_row, terms, last_raw, weights_all[:, :kv_at]),
    )
    item_part = lax.dynamic_slice_in_dim(embedded, me * share, share, 1)

    catalog = lax.all_to_all(copies, WIDE, 0, 0).reshape(-1, kv_at + share)

    wo_theirs, wo_mine = call(
        layout_kernel,
        "output_weights",
        20,
        [jax.ShapeDtypeStruct((n_x, share, wo_user.shape[0]), jnp.bfloat16)] * 2,
        [SMEM, VMEM],
        (scalars, weights_all),
    )
    slots = history_items.shape[1]
    user_mixed, theirs, residual = call(
        user_kernel,
        "user_attention",
        20,
        (
            jax.ShapeDtypeStruct((slots, heads_width), jnp.bfloat16),
            jax.ShapeDtypeStruct((n_x, slots, share), jnp.bfloat16),
            jax.ShapeDtypeStruct((slots, share), jnp.bfloat16),
        ),
        [SMEM] + [VMEM] * 3,
        (scalars, places, catalog, wo_theirs),
        [pltpu.VMEM((slots, kv_at), jnp.bfloat16)],
    )

    theirs = swap_cores(theirs)
    first, direct, second, own = call(
        pair_kernel,
        "pair_sum",
        20,
        [jax.ShapeDtypeStruct((slots, share), jnp.bfloat16)] * n_x,
        [VMEM] * 3,
        (user_mixed, wo_mine, theirs),
    )
    relay = along_x(first, 1)
    direct = along_x(direct, -1)
    relay = (relay.astype(jnp.float32) + second.astype(jnp.float32)).astype(jnp.bfloat16)
    relay = along_x(relay, 1)
    summed = own.astype(jnp.float32) + direct.astype(jnp.float32) + relay.astype(jnp.float32)
    live = (jnp.arange(slots, dtype=jnp.int32) < length)[:, None]
    user_states = jnp.where(live, residual.astype(jnp.float32) + summed, 0.0).astype(jnp.bfloat16)
    return (item_part, user_states)


def solution(mesh):
    n_wide, n_narrow = mesh.shape["wide"], mesh.shape["narrow"]
    side = math.isqrt(n_wide)
    fine = Mesh(
        mesh.devices.reshape(side, n_wide // side, n_narrow // 2, 2), WIDE + NARROW
    )
    return jax.shard_map(
        local,
        mesh=fine,
        in_specs=(
            P(WIDE + NARROW, None),
            P(),
            P(None, NARROW),
            P(None, NARROW, None),
            P(NARROW, None),
            P(),
            P(WIDE, NARROW),
            P(WIDE, NARROW, None),
            P(NARROW, WIDE),
            P(WIDE, None),
            P(WIDE),
        ),
        out_specs=(P(WIDE, NARROW), P(WIDE, NARROW)),
        check_vma=False,
    )
```

```python
import math

import jax
import jax.numpy as jnp
from jax import lax
from jax.experimental import pallas as pl
from jax.experimental.pallas import tpu as pltpu
from jax.sharding import Mesh
from jax.sharding import PartitionSpec as P

HEAD_DIM = 64
TXT = 128
epsilon = 1e-05
MIB = 1024 * 1024
WIDE = ("y", "z")
NARROW = ("x", "core")


def rms_scale(values, gain):
    wide = values.astype(jnp.float32)
    power = jnp.mean(wide * wide, axis=-1, keepdims=True)
    return (wide * lax.rsqrt(power + epsilon) * gain.astype(jnp.float32)).astype(jnp.bfloat16)


def dot_t(left, right):
    return lax.dot_general(
        left, right, (((1,), (1,)), ((), ())), preferred_element_type=jnp.float32
    )


def spread(values, axis):
    copies = jnp.broadcast_to(values[None], (lax.axis_size(axis),) + values.shape)
    return lax.all_to_all(copies, axis, 0, 0)


def swap_cores(values):
    return lax.ppermute(values, "core", [(0, 1), (1, 0)])


def along_x(values, step):
    n_x = lax.axis_size("x")
    pairs = [
        (2 * x + core, 2 * ((x + step * (1 - 2 * core)) % n_x) + core)
        for x in range(n_x)
        for core in range(2)
    ]
    return lax.ppermute(values, NARROW, pairs)


def load(source, target, sem):
    copy = pltpu.make_async_copy(source, target, sem)
    copy.start()
    return copy


def first_kernel(wq_ref, wkv_ref, wo_ref, copies_ref, sems):
    at, loads = 0, []
    for k, ref in enumerate((wq_ref, wkv_ref, wo_ref)):
        columns = ref.shape[1]
        loads.append(load(ref, copies_ref.at[0, :, pl.ds(at, columns)], sems.at[k]))
        at += columns
    for copy in loads:
        copy.wait()
    for k in range(1, copies_ref.shape[0]):
        copies_ref[k] = copies_ref[0]


def message_kernel(states_ref, message_ref, tail_ref, sem):
    tail = tail_ref.shape[0]
    load(states_ref.at[pl.ds(TXT - tail, tail)], tail_ref, sem).wait()
    row = tail_ref[...].astype(jnp.float32)[-1:]
    pieces, share = message_ref.shape[1:]
    tile = jnp.concatenate([row[:, j * share : (j + 1) * share] for j in range(pieces)], axis=0)
    for k in range(message_ref.shape[0]):
        message_ref[k] = tile


def probe_kernel(gain_ref, last_ref, wq_ref, wkv_ref, probes_ref, raw_ref):
    raw = jnp.concatenate([last_ref[:, j, :] for j in range(last_ref.shape[1])], axis=1)
    raw_ref[...] = raw
    power = jnp.mean(raw * raw, axis=-1, keepdims=True)
    normed = raw * lax.rsqrt(power + epsilon) * gain_ref[...].astype(jnp.float32)
    queries = jnp.dot(normed.astype(jnp.bfloat16), wq_ref[...], preferred_element_type=jnp.float32)
    queries = queries.astype(jnp.bfloat16)
    keys = wkv_ref[:, :HEAD_DIM]
    for head in range(probes_ref.shape[1]):
        lanes = slice(head * HEAD_DIM, (head + 1) * HEAD_DIM)
        probes_ref[:, head, :] = dot_t(queries[:, lanes], keys).astype(jnp.bfloat16)


def pool_kernel(probes_ref, normed_ref, pooled_ref):
    items, per = probes_ref.shape[:2]
    probes = jnp.concatenate([probes_ref[k].astype(jnp.float32) for k in range(items)], axis=0)
    scores = dot_t(probes.astype(jnp.bfloat16), normed_ref[...]) * (1.0 / math.sqrt(HEAD_DIM))
    parts = jnp.exp(scores - jnp.max(scores, axis=1, keepdims=True))
    parts = parts / jnp.sum(parts, axis=1, keepdims=True)
    pooled = jnp.dot(parts.astype(jnp.bfloat16), normed_ref[...], preferred_element_type=jnp.float32)
    for k in range(items):
        pooled_ref[k] = pooled[k * per : (k + 1) * per].astype(jnp.bfloat16)


def embed_kernel(gain_ref, terms_ref, last_ref, embedded_ref, normed_ref):
    total = last_ref[...]
    for k in range(terms_ref.shape[0]):
        total = total + terms_ref[k].astype(jnp.float32)
    embedded = total.astype(jnp.bfloat16)
    embedded_ref[...] = embedded
    wide = embedded.astype(jnp.float32)
    power = jnp.mean(wide * wide, axis=-1, keepdims=True)
    normed = wide * lax.rsqrt(power + epsilon) * gain_ref[...].astype(jnp.float32)
    normed_ref[...] = normed.astype(jnp.bfloat16)


def layout_kernel(scalar_ref, weights_ref, theirs_ref, mine_ref):
    n_x, share, out_width = mine_ref.shape
    core, place = scalar_ref[1], scalar_ref[2]
    step = 1 - 2 * core
    for k, (theirs, mine) in enumerate(((2, 2), (step, -step), (-step, step), (0, 0))):
        rows = (2 * lax.rem(place + n_x + theirs, n_x) + 1 - core) * share
        rows = pl.ds(pl.multiple_of(rows, share), share)
        theirs_ref[k] = weights_ref[rows, -out_width:]
        rows = (2 * lax.rem(place + n_x + mine, n_x) + core) * share
        rows = pl.ds(pl.multiple_of(rows, share), share)
        mine_ref[k] = weights_ref[rows, -out_width:]


def user_kernel(
    scalar_ref, places_ref, catalog_ref, mixed_ref, residual_ref, picked_ref
):
    length = scalar_ref[0]
    slots, q_width = mixed_ref.shape
    catalog, kv_at = catalog_ref.shape[0], q_width + 2 * HEAD_DIM
    every = lax.broadcasted_iota(jnp.int32, (slots, catalog), 1)
    picks = jnp.where(places_ref[...] == every, 1.0, 0.0).astype(jnp.bfloat16)
    picked = jnp.dot(picks, catalog_ref[...], preferred_element_type=jnp.float32)
    picked_ref[...] = picked[:, :kv_at].astype(jnp.bfloat16)
    residual_ref[...] = picked[:, kv_at:].astype(jnp.bfloat16)
    scale = 1.0 / math.sqrt(HEAD_DIM)
    chunk = min(slots, 256)
    for start in range(0, slots, chunk):
        upto = start + chunk
        keys = picked_ref[:upto, q_width : q_width + HEAD_DIM]
        values = picked_ref[:upto, q_width + HEAD_DIM : kv_at]
        row = start + lax.broadcasted_iota(jnp.int32, (chunk, upto), 0)
        column = lax.broadcasted_iota(jnp.int32, (chunk, upto), 1)
        allowed = (column <= row) & (column < length)
        for head in range(q_width // HEAD_DIM):
            lanes = slice(head * HEAD_DIM, (head + 1) * HEAD_DIM)
            scores = dot_t(picked_ref[start:upto, lanes], keys) * scale
            scores = jnp.where(allowed, scores, -1e30)
            top = jnp.max(scores, axis=1, keepdims=True)
            parts = jnp.exp(scores - top)
            total = jnp.sum(parts, axis=1, keepdims=True)
            mixed = jnp.dot(parts.astype(jnp.bfloat16), values, preferred_element_type=jnp.float32)
            mixed_ref[start:upto, lanes] = (mixed / total).astype(jnp.bfloat16)


def output_kernel(mine_ref, others_ref, wo_mine_ref, wo_others_ref, *block_refs):
    for k, ref in enumerate(block_refs):
        terms = dot_t(mine_ref[...], wo_mine_ref[k]) + dot_t(others_ref[...], wo_others_ref[k])
        ref[...] = terms.astype(jnp.bfloat16)


SMEM = pl.BlockSpec(memory_space=pltpu.SMEM)
VMEM = pl.BlockSpec(memory_space=pltpu.VMEM)
ANY = pl.BlockSpec(memory_space=pl.ANY)


def call(kernel, name, limit, outs, in_specs, ins, scratch=()):
    return pl.pallas_call(
        kernel,
        name=name,
        out_shape=outs,
        in_specs=in_specs,
        out_specs=jax.tree.map(lambda _: VMEM, outs),
        scratch_shapes=scratch,
        compiler_params=pltpu.CompilerParams(vmem_limit_bytes=limit * MIB),
    )(*ins)


def local(
    item_states,
    item_gain,
    wq_item,
    wkv_item,
    wo_item,
    user_gain,
    wq_user,
    wkv_user,
    wo_user,
    history_items,
    history_lengths,
):
    width = item_states.shape[1]
    n_x = lax.axis_size("x")
    n_narrow = 2 * n_x
    share = width // n_narrow
    core = lax.axis_index("core")
    me = lax.axis_index("x") * 2 + core
    scale = 1.0 / math.sqrt(HEAD_DIM)

    columns = wq_user.shape[1] + 2 * HEAD_DIM + wo_user.shape[0]
    n_z = lax.axis_size("z")
    depth, heads_width = wq_user.shape
    kv_at = heads_width + 2 * HEAD_DIM
    columns = kv_at + wo_user.shape[0]
    copies = call(
        first_kernel,
        "user_weights",
        60,
        jax.ShapeDtypeStruct((n_z, depth, columns), jnp.bfloat16),
        [ANY] * 3,
        (wq_user, wkv_user.reshape(depth, -1), wo_user.T),
        [pltpu.SemaphoreType.DMA((3,))],
    )
    weights_z = lax.all_to_all(copies, "z", 0, 0).reshape(n_z * depth, columns)
    messages = call(
        message_kernel,
        "last_rows",
        20,
        jax.ShapeDtypeStruct((n_narrow, n_narrow, share), jnp.float32),
        [ANY],
        (item_states,),
        [pltpu.VMEM((16, width), jnp.bfloat16), pltpu.SemaphoreType.DMA],
    )
    length = history_lengths[0]
    weights_z, messages, normed, places, scalars, gain_row, item_gain_row = (
        lax.optimization_barrier(
            (
                weights_z,
                messages,
                rms_scale(item_states, item_gain),
                history_items[0][:, None],
                jnp.stack([length, core, lax.axis_index("x")]).astype(jnp.int32),
                user_gain[None],
                item_gain[None],
            )
        )
    )
    weights_all = lax.all_gather(weights_z, "y", axis=0, tiled=True)
    last_raw = lax.all_to_all(messages, NARROW, 0, 0)
    per = wq_item.shape[1] // HEAD_DIM
    wkv = wkv_item.reshape(width, -1)
    wv = wkv[:, HEAD_DIM:]
    probes, last_raw = call(
        probe_kernel,
        "item_probes",
        20,
        (
            jax.ShapeDtypeStruct((n_narrow, per, width), jnp.bfloat16),
            jax.ShapeDtypeStruct((n_narrow, width), jnp.float32),
        ),
        [VMEM] * 4,
        (item_gain_row, last_raw, wq_item, wkv),
    )
    probes = lax.all_to_all(probes, NARROW, 0, 0)
    pooled = call(
        pool_kernel,
        "item_attention",
        20,
        jax.ShapeDtypeStruct(probes.shape, jnp.bfloat16),
        [VMEM] * 2,
        (probes, normed),
    )
    pooled = lax.all_to_all(pooled, NARROW, 0, 0)
    mixed = jnp.dot(pooled.reshape(-1, width), wv, preferred_element_type=jnp.float32)
    mixed = mixed.astype(jnp.bfloat16).reshape(n_narrow, -1)
    partial_sum = jnp.dot(mixed, wo_item, preferred_element_type=jnp.float32)
    terms = spread(partial_sum.astype(jnp.bfloat16), NARROW)
    group = terms.shape[1]
    embedded, items_normed = call(
        embed_kernel,
        "item_embeddings",
        20,
        [jax.ShapeDtypeStruct((group, width), jnp.bfloat16)] * 2,
        [VMEM] * 3,
        (gain_row, terms, last_raw),
    )
    item_part = lax.dynamic_slice_in_dim(embedded, me * share, share, 1)
    projected = jnp.dot(
        items_normed, weights_all[:, :kv_at], preferred_element_type=jnp.float32
    ).astype(jnp.bfloat16)
    projected = jnp.concatenate([projected, item_part], axis=1)

    catalog = spread(projected, WIDE).reshape(-1, kv_at + share)

    wo_theirs, wo_mine = call(
        layout_kernel,
        "output_weights",
        20,
        [jax.ShapeDtypeStruct((n_x, share, wo_user.shape[0]), jnp.bfloat16)] * 2,
        [SMEM, VMEM],
        (scalars, weights_all),
    )
    wo_others = swap_cores(wo_theirs)
    slots = history_items.shape[1]
    user_mixed, residual = call(
        user_kernel,
        "user_attention",
        20,
        (
            jax.ShapeDtypeStruct((slots, heads_width), jnp.bfloat16),
            jax.ShapeDtypeStruct((slots, share), jnp.bfloat16),
        ),
        [SMEM] + [VMEM] * 2,
        (scalars, places, catalog),
        [pltpu.VMEM((slots, kv_at), jnp.bfloat16)],
    )

    first, direct, second, own = call(
        output_kernel,
        "output_blocks",
        20,
        [jax.ShapeDtypeStruct((slots, share), jnp.bfloat16)] * n_x,
        [VMEM] * 4,
        (user_mixed, swap_cores(user_mixed), wo_mine, wo_others),
    )
    relay = along_x(first, 1)
    direct = along_x(direct, -1)
    relay = (relay.astype(jnp.float32) + second.astype(jnp.float32)).astype(jnp.bfloat16)
    relay = along_x(relay, 1)
    summed = own.astype(jnp.float32) + direct.astype(jnp.float32) + relay.astype(jnp.float32)
    live = (jnp.arange(slots, dtype=jnp.int32) < length)[:, None]
    user_states = jnp.where(live, residual.astype(jnp.float32) + summed, 0.0).astype(jnp.bfloat16)
    return (item_part, user_states)


def solution(mesh):
    n_wide, n_narrow = mesh.shape["wide"], mesh.shape["narrow"]
    side = math.isqrt(n_wide)
    fine = Mesh(
        mesh.devices.reshape(side, n_wide // side, n_narrow // 2, 2), WIDE + NARROW
    )
    return jax.shard_map(
        local,
        mesh=fine,
        in_specs=(
            P(WIDE + NARROW, None),
            P(),
            P(None, NARROW),
            P(None, NARROW, None),
            P(NARROW, None),
            P(),
            P(WIDE, NARROW),
            P(WIDE, NARROW, None),
            P(NARROW, WIDE),
            P(WIDE, None),
            P(WIDE),
        ),
        out_specs=(P(WIDE, NARROW), P(WIDE, NARROW)),
        check_vma=False,
    )
```

```python
import math

import jax
import jax.numpy as jnp
from jax import lax
from jax.experimental import pallas as pl
from jax.experimental.pallas import tpu as pltpu
from jax.sharding import Mesh
from jax.sharding import PartitionSpec as P

HEAD_DIM = 64
TXT = 128
epsilon = 1e-05
MIB = 1024 * 1024
WIDE = ("y", "z")
NARROW = ("x", "core")


def rms_scale(values, gain):
    wide = values.astype(jnp.float32)
    power = jnp.mean(wide * wide, axis=-1, keepdims=True)
    return (wide * lax.rsqrt(power + epsilon) * gain.astype(jnp.float32)).astype(jnp.bfloat16)


def dot_t(left, right):
    return lax.dot_general(
        left, right, (((1,), (1,)), ((), ())), preferred_element_type=jnp.float32
    )


def spread(values, axis):
    copies = jnp.broadcast_to(values[None], (lax.axis_size(axis),) + values.shape)
    return lax.all_to_all(copies, axis, 0, 0)


def swap_cores(values):
    return lax.ppermute(values, "core", [(0, 1), (1, 0)])


def along_x(values, step):
    n_x = lax.axis_size("x")
    pairs = [
        (2 * x + core, 2 * ((x + step * (1 - 2 * core)) % n_x) + core)
        for x in range(n_x)
        for core in range(2)
    ]
    return lax.ppermute(values, NARROW, pairs)


def load(source, target, sem):
    copy = pltpu.make_async_copy(source, target, sem)
    copy.start()
    return copy


def first_kernel(wq_ref, wkv_ref, wo_ref, copies_ref, sems):
    at, loads = 0, []
    for k, ref in enumerate((wq_ref, wkv_ref, wo_ref)):
        columns = ref.shape[1]
        loads.append(load(ref, copies_ref.at[0, :, pl.ds(at, columns)], sems.at[k]))
        at += columns
    for copy in loads:
        copy.wait()
    for k in range(1, copies_ref.shape[0]):
        copies_ref[k] = copies_ref[0]


def message_kernel(states_ref, message_ref, tail_ref, sem):
    tail = tail_ref.shape[0]
    load(states_ref.at[pl.ds(TXT - tail, tail)], tail_ref, sem).wait()
    row = tail_ref[...].astype(jnp.float32)[-1:]
    pieces, share = message_ref.shape[1:]
    tile = jnp.concatenate([row[:, j * share : (j + 1) * share] for j in range(pieces)], axis=0)
    for k in range(message_ref.shape[0]):
        message_ref[k] = tile


def probe_kernel(gain_ref, last_ref, wq_ref, wkv_ref, probes_ref, raw_ref):
    raw = jnp.concatenate([last_ref[:, j, :] for j in range(last_ref.shape[1])], axis=1)
    raw_ref[...] = raw
    power = jnp.mean(raw * raw, axis=-1, keepdims=True)
    normed = raw * lax.rsqrt(power + epsilon) * gain_ref[...].astype(jnp.float32)
    queries = jnp.dot(normed.astype(jnp.bfloat16), wq_ref[...], preferred_element_type=jnp.float32)
    queries = queries.astype(jnp.bfloat16)
    keys = wkv_ref[:, :HEAD_DIM]
    for head in range(probes_ref.shape[1]):
        lanes = slice(head * HEAD_DIM, (head + 1) * HEAD_DIM)
        probes_ref[:, head, :] = dot_t(queries[:, lanes], keys).astype(jnp.bfloat16)


def pool_kernel(probes_ref, normed_ref, pooled_ref):
    items, per = probes_ref.shape[:2]
    probes = jnp.concatenate([probes_ref[k].astype(jnp.float32) for k in range(items)], axis=0)
    scores = dot_t(probes.astype(jnp.bfloat16), normed_ref[...]) * (1.0 / math.sqrt(HEAD_DIM))
    parts = jnp.exp(scores - jnp.max(scores, axis=1, keepdims=True))
    parts = parts / jnp.sum(parts, axis=1, keepdims=True)
    pooled = jnp.dot(parts.astype(jnp.bfloat16), normed_ref[...], preferred_element_type=jnp.float32)
    for k in range(items):
        pooled_ref[k] = pooled[k * per : (k + 1) * per].astype(jnp.bfloat16)


def embed_kernel(gain_ref, terms_ref, last_ref, embedded_ref, normed_ref):
    total = last_ref[...]
    for k in range(terms_ref.shape[0]):
        total = total + terms_ref[k].astype(jnp.float32)
    embedded = total.astype(jnp.bfloat16)
    embedded_ref[...] = embedded
    wide = embedded.astype(jnp.float32)
    power = jnp.mean(wide * wide, axis=-1, keepdims=True)
    normed = wide * lax.rsqrt(power + epsilon) * gain_ref[...].astype(jnp.float32)
    normed_ref[...] = normed.astype(jnp.bfloat16)


def layout_kernel(scalar_ref, weights_ref, theirs_ref, mine_ref):
    n_x, share, out_width = mine_ref.shape
    core, place = scalar_ref[1], scalar_ref[2]
    step = 1 - 2 * core
    for k, (theirs, mine) in enumerate(((2, 2), (step, -step), (-step, step), (0, 0))):
        rows = (2 * lax.rem(place + n_x + theirs, n_x) + 1 - core) * share
        rows = pl.ds(pl.multiple_of(rows, share), share)
        theirs_ref[k] = weights_ref[rows, -out_width:]
        rows = (2 * lax.rem(place + n_x + mine, n_x) + core) * share
        rows = pl.ds(pl.multiple_of(rows, share), share)
        mine_ref[k] = weights_ref[rows, -out_width:]


def user_kernel(
    scalar_ref, places_ref, catalog_ref, mixed_ref, residual_ref, query_ref, key_ref, value_ref
):
    length = scalar_ref[0]
    slots, q_width = mixed_ref.shape
    catalog, kv_at = catalog_ref.shape[0], q_width + 2 * HEAD_DIM
    every = lax.broadcasted_iota(jnp.int32, (slots, catalog), 1)
    picks = jnp.where(places_ref[...] == every, 1.0, 0.0).astype(jnp.bfloat16)
    picked = jnp.dot(picks, catalog_ref[...], preferred_element_type=jnp.float32)
    scale = 1.0 / math.sqrt(HEAD_DIM)
    query_ref[...] = (picked[:, :q_width] * scale).astype(jnp.bfloat16)
    key_ref[...] = picked[:, q_width : q_width + HEAD_DIM].astype(jnp.bfloat16)
    values = picked[:, q_width + HEAD_DIM : kv_at]
    value_ref[...] = jnp.concatenate([values, jnp.ones_like(values)], axis=1).astype(jnp.bfloat16)
    residual_ref[...] = picked[:, kv_at:].astype(jnp.bfloat16)
    chunk = min(slots, 256)
    for start in range(0, slots, chunk):
        upto = start + chunk
        row = start + lax.broadcasted_iota(jnp.int32, (chunk, upto), 0)
        column = lax.broadcasted_iota(jnp.int32, (chunk, upto), 1)
        allowed = (column <= row) & (column < length)
        for head in range(q_width // HEAD_DIM):
            lanes = slice(head * HEAD_DIM, (head + 1) * HEAD_DIM)
            scores = dot_t(query_ref[start:upto, lanes], key_ref[:upto, :])
            scores = jnp.where(allowed, scores, -1e30)
            parts = jnp.exp(scores - jnp.max(scores, axis=1, keepdims=True))
            mixed = jnp.dot(
                parts.astype(jnp.bfloat16), value_ref[:upto, :], preferred_element_type=jnp.float32
            )
            mixed = mixed[:, :HEAD_DIM] / mixed[:, HEAD_DIM:]
            mixed_ref[start:upto, lanes] = mixed.astype(jnp.bfloat16)


def output_kernel(mine_ref, others_ref, wo_mine_ref, wo_others_ref, *block_refs):
    skip = wo_mine_ref.shape[0] - len(block_refs)
    for k, ref in enumerate(block_refs):
        terms = dot_t(mine_ref[...], wo_mine_ref[skip + k])
        terms += dot_t(others_ref[...], wo_others_ref[skip + k])
        ref[...] = terms.astype(jnp.bfloat16)


def first_output_kernel(mine_ref, others_ref, wo_mine_ref, wo_others_ref, block_ref):
    terms = dot_t(mine_ref[...], wo_mine_ref[0]) + dot_t(others_ref[...], wo_others_ref[0])
    block_ref[...] = terms.astype(jnp.bfloat16)


SMEM = pl.BlockSpec(memory_space=pltpu.SMEM)
VMEM = pl.BlockSpec(memory_space=pltpu.VMEM)
ANY = pl.BlockSpec(memory_space=pl.ANY)


def call(kernel, name, limit, outs, in_specs, ins, scratch=()):
    return pl.pallas_call(
        kernel,
        name=name,
        out_shape=outs,
        in_specs=in_specs,
        out_specs=jax.tree.map(lambda _: VMEM, outs),
        scratch_shapes=scratch,
        compiler_params=pltpu.CompilerParams(vmem_limit_bytes=limit * MIB),
    )(*ins)


def local(
    item_states,
    item_gain,
    wq_item,
    wkv_item,
    wo_item,
    user_gain,
    wq_user,
    wkv_user,
    wo_user,
    history_items,
    history_lengths,
):
    width = item_states.shape[1]
    n_x = lax.axis_size("x")
    n_narrow = 2 * n_x
    share = width // n_narrow
    core = lax.axis_index("core")
    me = lax.axis_index("x") * 2 + core
    scale = 1.0 / math.sqrt(HEAD_DIM)

    columns = wq_user.shape[1] + 2 * HEAD_DIM + wo_user.shape[0]
    n_z = lax.axis_size("z")
    depth, heads_width = wq_user.shape
    kv_at = heads_width + 2 * HEAD_DIM
    columns = kv_at + wo_user.shape[0]
    copies = call(
        first_kernel,
        "user_weights",
        60,
        jax.ShapeDtypeStruct((n_z, depth, columns), jnp.bfloat16),
        [ANY] * 3,
        (wq_user, wkv_user.reshape(depth, -1), wo_user.T),
        [pltpu.SemaphoreType.DMA((3,))],
    )
    weights_z = lax.all_to_all(copies, "z", 0, 0).reshape(n_z * depth, columns)
    messages = call(
        message_kernel,
        "last_rows",
        20,
        jax.ShapeDtypeStruct((n_narrow, n_narrow, share), jnp.float32),
        [ANY],
        (item_states,),
        [pltpu.VMEM((16, width), jnp.bfloat16), pltpu.SemaphoreType.DMA],
    )
    length = history_lengths[0]
    weights_z, messages, normed, places, scalars, gain_row, item_gain_row = (
        lax.optimization_barrier(
            (
                weights_z,
                messages,
                rms_scale(item_states, item_gain),
                history_items[0][:, None],
                jnp.stack([length, core, lax.axis_index("x")]).astype(jnp.int32),
                user_gain[None],
                item_gain[None],
            )
        )
    )
    weights_all = lax.all_gather(weights_z, "y", axis=0, tiled=True)
    last_raw = lax.all_to_all(messages, NARROW, 0, 0)
    per = wq_item.shape[1] // HEAD_DIM
    wkv = wkv_item.reshape(width, -1)
    wv = wkv[:, HEAD_DIM:]
    probes, last_raw = call(
        probe_kernel,
        "item_probes",
        20,
        (
            jax.ShapeDtypeStruct((n_narrow, per, width), jnp.bfloat16),
            jax.ShapeDtypeStruct((n_narrow, width), jnp.float32),
        ),
        [VMEM] * 4,
        (item_gain_row, last_raw, wq_item, wkv),
    )
    probes = lax.all_to_all(probes, NARROW, 0, 0)
    pooled = call(
        pool_kernel,
        "item_attention",
        20,
        jax.ShapeDtypeStruct(probes.shape, jnp.bfloat16),
        [VMEM] * 2,
        (probes, normed),
    )
    pooled = lax.all_to_all(pooled, NARROW, 0, 0)
    mixed = jnp.dot(pooled.reshape(-1, width), wv, preferred_element_type=jnp.float32)
    mixed = mixed.astype(jnp.bfloat16).reshape(n_narrow, -1)
    partial_sum = jnp.dot(mixed, wo_item, preferred_element_type=jnp.float32)
    terms = spread(partial_sum.astype(jnp.bfloat16), NARROW)
    group = terms.shape[1]
    embedded, items_normed = call(
        embed_kernel,
        "item_embeddings",
        20,
        [jax.ShapeDtypeStruct((group, width), jnp.bfloat16)] * 2,
        [VMEM] * 3,
        (gain_row, terms, last_raw),
    )
    item_part = lax.dynamic_slice_in_dim(embedded, me * share, share, 1)
    projected = jnp.dot(
        items_normed, weights_all[:, :kv_at], preferred_element_type=jnp.float32
    ).astype(jnp.bfloat16)
    projected = jnp.concatenate([projected, item_part], axis=1)

    catalog = spread(projected, WIDE).reshape(-1, kv_at + share)

    wo_theirs, wo_mine = call(
        layout_kernel,
        "output_weights",
        20,
        [jax.ShapeDtypeStruct((n_x, share, wo_user.shape[0]), jnp.bfloat16)] * 2,
        [SMEM, VMEM],
        (scalars, weights_all),
    )
    wo_others = swap_cores(wo_theirs)
    slots = history_items.shape[1]
    user_mixed, residual = call(
        user_kernel,
        "user_attention",
        20,
        (
            jax.ShapeDtypeStruct((slots, heads_width), jnp.bfloat16),
            jax.ShapeDtypeStruct((slots, share), jnp.bfloat16),
        ),
        [SMEM] + [VMEM] * 2,
        (scalars, places, catalog),
        [
            pltpu.VMEM((slots, heads_width), jnp.bfloat16),
            pltpu.VMEM((slots, HEAD_DIM), jnp.bfloat16),
            pltpu.VMEM((slots, 2 * HEAD_DIM), jnp.bfloat16),
        ],
    )

    block = jax.ShapeDtypeStruct((slots, share), jnp.bfloat16)
    operands = (user_mixed, swap_cores(user_mixed), wo_mine, wo_others)
    first = call(first_output_kernel, "output_first", 20, block, [VMEM] * 4, operands)
    direct, second, own = call(
        output_kernel, "output_blocks", 20, [block] * (n_x - 1), [VMEM] * 4, operands
    )
    relay = along_x(first, 1)
    direct = along_x(direct, -1)
    relay = (relay.astype(jnp.float32) + second.astype(jnp.float32)).astype(jnp.bfloat16)
    relay = along_x(relay, 1)
    live = (jnp.arange(slots, dtype=jnp.int32) < length)[:, None]
    summed = residual.astype(jnp.float32) + own.astype(jnp.float32) + direct.astype(jnp.float32)
    summed = lax.optimization_barrier(summed) + relay.astype(jnp.float32)
    user_states = jnp.where(live, summed, 0.0).astype(jnp.bfloat16)
    return (item_part, user_states)


def solution(mesh):
    n_wide, n_narrow = mesh.shape["wide"], mesh.shape["narrow"]
    side = math.isqrt(n_wide)
    fine = Mesh(
        mesh.devices.reshape(side, n_wide // side, n_narrow // 2, 2), WIDE + NARROW
    )
    return jax.shard_map(
        local,
        mesh=fine,
        in_specs=(
            P(WIDE + NARROW, None),
            P(),
            P(None, NARROW),
            P(None, NARROW, None),
            P(NARROW, None),
            P(),
            P(WIDE, NARROW),
            P(WIDE, NARROW, None),
            P(NARROW, WIDE),
            P(WIDE, None),
            P(WIDE),
        ),
        out_specs=(P(WIDE, NARROW), P(WIDE, NARROW)),
        check_vma=False,
    )
```

```python
import math

import jax
import jax.numpy as jnp
from jax import lax
from jax.experimental import pallas as pl
from jax.experimental.pallas import tpu as pltpu
from jax.sharding import Mesh
from jax.sharding import PartitionSpec as P

HEAD_DIM = 64
TXT = 128
epsilon = 1e-05
MIB = 1024 * 1024
WIDE = ("y", "z")
NARROW = ("x", "core")


def rms_scale(values, gain):
    wide = values.astype(jnp.float32)
    power = jnp.mean(wide * wide, axis=-1, keepdims=True)
    return (wide * lax.rsqrt(power + epsilon) * gain.astype(jnp.float32)).astype(jnp.bfloat16)


def dot_t(left, right):
    return lax.dot_general(
        left, right, (((1,), (1,)), ((), ())), preferred_element_type=jnp.float32
    )


def spread(values, axis):
    copies = jnp.broadcast_to(values[None], (lax.axis_size(axis),) + values.shape)
    return lax.all_to_all(copies, axis, 0, 0)


def swap_cores(values):
    return lax.ppermute(values, "core", [(0, 1), (1, 0)])


def along_x(values, step):
    n_x = lax.axis_size("x")
    pairs = [
        (2 * x + core, 2 * ((x + step * (1 - 2 * core)) % n_x) + core)
        for x in range(n_x)
        for core in range(2)
    ]
    return lax.ppermute(values, NARROW, pairs)


def load(source, target, sem):
    copy = pltpu.make_async_copy(source, target, sem)
    copy.start()
    return copy


def first_kernel(wq_ref, wkv_ref, wo_ref, copies_ref, sems):
    at, loads = 0, []
    for k, ref in enumerate((wq_ref, wkv_ref, wo_ref)):
        columns = ref.shape[1]
        loads.append(load(ref, copies_ref.at[0, :, pl.ds(at, columns)], sems.at[k]))
        at += columns
    for copy in loads:
        copy.wait()
    for k in range(1, copies_ref.shape[0]):
        copies_ref[k] = copies_ref[0]


def message_kernel(states_ref, message_ref, tail_ref, sem):
    tail = tail_ref.shape[0]
    load(states_ref.at[pl.ds(TXT - tail, tail)], tail_ref, sem).wait()
    row = tail_ref[...].astype(jnp.float32)[-1:]
    pieces, share = message_ref.shape[1:]
    tile = jnp.concatenate([row[:, j * share : (j + 1) * share] for j in range(pieces)], axis=0)
    for k in range(message_ref.shape[0]):
        message_ref[k] = tile


def probe_kernel(gain_ref, last_ref, wq_ref, wkv_ref, probes_ref, raw_ref):
    raw = jnp.concatenate([last_ref[:, j, :] for j in range(last_ref.shape[1])], axis=1)
    raw_ref[...] = raw
    power = jnp.mean(raw * raw, axis=-1, keepdims=True)
    normed = raw * lax.rsqrt(power + epsilon) * gain_ref[...].astype(jnp.float32)
    queries = jnp.dot(normed.astype(jnp.bfloat16), wq_ref[...], preferred_element_type=jnp.float32)
    queries = queries.astype(jnp.bfloat16)
    keys = wkv_ref[:, :HEAD_DIM]
    for head in range(probes_ref.shape[1]):
        lanes = slice(head * HEAD_DIM, (head + 1) * HEAD_DIM)
        probes_ref[:, head, :] = dot_t(queries[:, lanes], keys).astype(jnp.bfloat16)


def pool_kernel(probes_ref, normed_ref, pooled_ref):
    items, per = probes_ref.shape[:2]
    probes = jnp.concatenate([probes_ref[k].astype(jnp.float32) for k in range(items)], axis=0)
    scores = dot_t(probes.astype(jnp.bfloat16), normed_ref[...]) * (1.0 / math.sqrt(HEAD_DIM))
    parts = jnp.exp(scores - jnp.max(scores, axis=1, keepdims=True))
    parts = parts / jnp.sum(parts, axis=1, keepdims=True)
    pooled = jnp.dot(parts.astype(jnp.bfloat16), normed_ref[...], preferred_element_type=jnp.float32)
    for k in range(items):
        pooled_ref[k] = pooled[k * per : (k + 1) * per].astype(jnp.bfloat16)


def embed_kernel(gain_ref, terms_ref, last_ref, embedded_ref, normed_ref):
    total = last_ref[...]
    for k in range(terms_ref.shape[0]):
        total = total + terms_ref[k].astype(jnp.float32)
    embedded = total.astype(jnp.bfloat16)
    embedded_ref[...] = embedded
    wide = embedded.astype(jnp.float32)
    power = jnp.mean(wide * wide, axis=-1, keepdims=True)
    normed = wide * lax.rsqrt(power + epsilon) * gain_ref[...].astype(jnp.float32)
    normed_ref[...] = normed.astype(jnp.bfloat16)


def layout_kernel(scalar_ref, weights_ref, theirs_ref, mine_ref):
    n_x, share, out_width = mine_ref.shape
    core, place = scalar_ref[1], scalar_ref[2]
    step = 1 - 2 * core
    for k, (theirs, mine) in enumerate(((2, 2), (step, -step), (-step, step), (0, 0))):
        rows = (2 * lax.rem(place + n_x + theirs, n_x) + 1 - core) * share
        rows = pl.ds(pl.multiple_of(rows, share), share)
        theirs_ref[k] = weights_ref[rows, -out_width:]
        rows = (2 * lax.rem(place + n_x + mine, n_x) + core) * share
        rows = pl.ds(pl.multiple_of(rows, share), share)
        mine_ref[k] = weights_ref[rows, -out_width:]


def user_kernel(
    scalar_ref, places_ref, catalog_ref, mixed_ref, residual_ref, query_ref, key_ref, value_ref
):
    length = scalar_ref[0]
    slots, q_width = mixed_ref.shape
    catalog, kv_at = catalog_ref.shape[0], q_width + 2 * HEAD_DIM
    every = lax.broadcasted_iota(jnp.int32, (slots, catalog), 1)
    picks = jnp.where(places_ref[...] == every, 1.0, 0.0).astype(jnp.bfloat16)
    picked = jnp.dot(picks, catalog_ref[...], preferred_element_type=jnp.float32)
    scale = 1.0 / math.sqrt(HEAD_DIM)
    heads = q_width // HEAD_DIM
    for head in range(heads):
        lanes = slice(head * HEAD_DIM, (head + 1) * HEAD_DIM)
        query_ref[head] = (picked[:, lanes] * scale).astype(jnp.bfloat16)
    key_ref[...] = picked[:, q_width : q_width + HEAD_DIM].astype(jnp.bfloat16)
    values = picked[:, q_width + HEAD_DIM : kv_at]
    value_ref[...] = jnp.concatenate([values, jnp.ones_like(values)], axis=1).astype(jnp.bfloat16)
    residual_ref[...] = picked[:, kv_at:].astype(jnp.bfloat16)
    chunk = min(slots, 256)
    for start in range(0, slots, chunk):
        upto = start + chunk
        row = start + lax.broadcasted_iota(jnp.int32, (chunk, upto), 0)
        column = lax.broadcasted_iota(jnp.int32, (chunk, upto), 1)
        allowed = (column <= row) & (column < length)
        queries = query_ref[:, start:upto, :].reshape(heads * chunk, HEAD_DIM)
        scores = dot_t(queries, key_ref[:upto, :]).reshape(heads, chunk, upto)
        scores = jnp.where(allowed[None], scores, -1e30)
        parts = jnp.exp(scores - jnp.max(scores, axis=2, keepdims=True)).astype(jnp.bfloat16)
        mixed = jnp.dot(
            parts.reshape(heads * chunk, upto),
            value_ref[:upto, :],
            preferred_element_type=jnp.float32,
        )
        mixed = (mixed[:, :HEAD_DIM] / mixed[:, HEAD_DIM:]).astype(jnp.bfloat16)
        for head in range(heads):
            lanes = slice(head * HEAD_DIM, (head + 1) * HEAD_DIM)
            mixed_ref[start:upto, lanes] = mixed[head * chunk : (head + 1) * chunk]


def output_kernel(mine_ref, others_ref, wo_mine_ref, wo_others_ref, *block_refs):
    skip = wo_mine_ref.shape[0] - len(block_refs)
    for k, ref in enumerate(block_refs):
        terms = dot_t(mine_ref[...], wo_mine_ref[skip + k])
        terms += dot_t(others_ref[...], wo_others_ref[skip + k])
        ref[...] = terms.astype(jnp.bfloat16)


def first_output_kernel(mine_ref, others_ref, wo_mine_ref, wo_others_ref, block_ref):
    terms = dot_t(mine_ref[...], wo_mine_ref[0]) + dot_t(others_ref[...], wo_others_ref[0])
    block_ref[...] = terms.astype(jnp.bfloat16)


SMEM = pl.BlockSpec(memory_space=pltpu.SMEM)
VMEM = pl.BlockSpec(memory_space=pltpu.VMEM)
ANY = pl.BlockSpec(memory_space=pl.ANY)


def call(kernel, name, limit, outs, in_specs, ins, scratch=()):
    return pl.pallas_call(
        kernel,
        name=name,
        out_shape=outs,
        in_specs=in_specs,
        out_specs=jax.tree.map(lambda _: VMEM, outs),
        scratch_shapes=scratch,
        compiler_params=pltpu.CompilerParams(vmem_limit_bytes=limit * MIB),
    )(*ins)


def local(
    item_states,
    item_gain,
    wq_item,
    wkv_item,
    wo_item,
    user_gain,
    wq_user,
    wkv_user,
    wo_user,
    history_items,
    history_lengths,
):
    width = item_states.shape[1]
    n_x = lax.axis_size("x")
    n_narrow = 2 * n_x
    share = width // n_narrow
    core = lax.axis_index("core")
    me = lax.axis_index("x") * 2 + core
    scale = 1.0 / math.sqrt(HEAD_DIM)

    columns = wq_user.shape[1] + 2 * HEAD_DIM + wo_user.shape[0]
    n_z = lax.axis_size("z")
    depth, heads_width = wq_user.shape
    kv_at = heads_width + 2 * HEAD_DIM
    columns = kv_at + wo_user.shape[0]
    copies = call(
        first_kernel,
        "user_weights",
        60,
        jax.ShapeDtypeStruct((n_z, depth, columns), jnp.bfloat16),
        [ANY] * 3,
        (wq_user, wkv_user.reshape(depth, -1), wo_user.T),
        [pltpu.SemaphoreType.DMA((3,))],
    )
    weights_z = lax.all_to_all(copies, "z", 0, 0).reshape(n_z * depth, columns)
    messages = call(
        message_kernel,
        "last_rows",
        20,
        jax.ShapeDtypeStruct((n_narrow, n_narrow, share), jnp.float32),
        [ANY],
        (item_states,),
        [pltpu.VMEM((16, width), jnp.bfloat16), pltpu.SemaphoreType.DMA],
    )
    length = history_lengths[0]
    weights_z, messages, normed, places, scalars, gain_row, item_gain_row = (
        lax.optimization_barrier(
            (
                weights_z,
                messages,
                rms_scale(item_states, item_gain),
                history_items[0][:, None],
                jnp.stack([length, core, lax.axis_index("x")]).astype(jnp.int32),
                user_gain[None],
                item_gain[None],
            )
        )
    )
    weights_all = lax.all_gather(weights_z, "y", axis=0, tiled=True)
    last_raw = lax.all_to_all(messages, NARROW, 0, 0)
    per = wq_item.shape[1] // HEAD_DIM
    wkv = wkv_item.reshape(width, -1)
    wv = wkv[:, HEAD_DIM:]
    probes, last_raw = call(
        probe_kernel,
        "item_probes",
        20,
        (
            jax.ShapeDtypeStruct((n_narrow, per, width), jnp.bfloat16),
            jax.ShapeDtypeStruct((n_narrow, width), jnp.float32),
        ),
        [VMEM] * 4,
        (item_gain_row, last_raw, wq_item, wkv),
    )
    probes = lax.all_to_all(probes, NARROW, 0, 0)
    pooled = call(
        pool_kernel,
        "item_attention",
        20,
        jax.ShapeDtypeStruct(probes.shape, jnp.bfloat16),
        [VMEM] * 2,
        (probes, normed),
    )
    pooled = lax.all_to_all(pooled, NARROW, 0, 0)
    mixed = jnp.dot(pooled.reshape(-1, width), wv, preferred_element_type=jnp.float32)
    mixed = mixed.astype(jnp.bfloat16).reshape(n_narrow, -1)
    partial_sum = jnp.dot(mixed, wo_item, preferred_element_type=jnp.float32)
    terms = spread(partial_sum.astype(jnp.bfloat16), NARROW)
    group = terms.shape[1]
    embedded, items_normed = call(
        embed_kernel,
        "item_embeddings",
        20,
        [jax.ShapeDtypeStruct((group, width), jnp.bfloat16)] * 2,
        [VMEM] * 3,
        (gain_row, terms, last_raw),
    )
    item_part = lax.dynamic_slice_in_dim(embedded, me * share, share, 1)
    projected = jnp.dot(
        items_normed, weights_all[:, :kv_at], preferred_element_type=jnp.float32
    ).astype(jnp.bfloat16)
    projected = jnp.concatenate([projected, item_part], axis=1)

    catalog = spread(projected, WIDE).reshape(-1, kv_at + share)

    wo_theirs, wo_mine = call(
        layout_kernel,
        "output_weights",
        20,
        [jax.ShapeDtypeStruct((n_x, share, wo_user.shape[0]), jnp.bfloat16)] * 2,
        [SMEM, VMEM],
        (scalars, weights_all),
    )
    wo_others = swap_cores(wo_theirs)
    slots = history_items.shape[1]
    user_mixed, residual = call(
        user_kernel,
        "user_attention",
        20,
        (
            jax.ShapeDtypeStruct((slots, heads_width), jnp.bfloat16),
            jax.ShapeDtypeStruct((slots, share), jnp.bfloat16),
        ),
        [SMEM] + [VMEM] * 2,
        (scalars, places, catalog),
        [
            pltpu.VMEM((per, slots, HEAD_DIM), jnp.bfloat16),
            pltpu.VMEM((slots, HEAD_DIM), jnp.bfloat16),
            pltpu.VMEM((slots, 2 * HEAD_DIM), jnp.bfloat16),
        ],
    )

    block = jax.ShapeDtypeStruct((slots, share), jnp.bfloat16)
    operands = (user_mixed, swap_cores(user_mixed), wo_mine, wo_others)
    first = call(first_output_kernel, "output_first", 20, block, [VMEM] * 4, operands)
    direct, second, own = call(
        output_kernel, "output_blocks", 20, [block] * (n_x - 1), [VMEM] * 4, operands
    )
    relay = along_x(first, 1)
    direct = along_x(direct, -1)
    relay = (relay.astype(jnp.float32) + second.astype(jnp.float32)).astype(jnp.bfloat16)
    relay = along_x(relay, 1)
    live = (jnp.arange(slots, dtype=jnp.int32) < length)[:, None]
    summed = residual.astype(jnp.float32) + own.astype(jnp.float32) + direct.astype(jnp.float32)
    summed = lax.optimization_barrier(summed) + relay.astype(jnp.float32)
    user_states = jnp.where(live, summed, 0.0).astype(jnp.bfloat16)
    return (item_part, user_states)


def solution(mesh):
    n_wide, n_narrow = mesh.shape["wide"], mesh.shape["narrow"]
    side = math.isqrt(n_wide)
    fine = Mesh(
        mesh.devices.reshape(side, n_wide // side, n_narrow // 2, 2), WIDE + NARROW
    )
    return jax.shard_map(
        local,
        mesh=fine,
        in_specs=(
            P(WIDE + NARROW, None),
            P(),
            P(None, NARROW),
            P(None, NARROW, None),
            P(NARROW, None),
            P(),
            P(WIDE, NARROW),
            P(WIDE, NARROW, None),
            P(NARROW, WIDE),
            P(WIDE, None),
            P(WIDE),
        ),
        out_specs=(P(WIDE, NARROW), P(WIDE, NARROW)),
        check_vma=False,
    )
```

```python
import math

import jax
import jax.numpy as jnp
from jax import lax
from jax.experimental import pallas as pl
from jax.experimental.pallas import tpu as pltpu
from jax.sharding import Mesh
from jax.sharding import PartitionSpec as P

HEAD_DIM = 64
TXT = 128
epsilon = 1e-05
MIB = 1024 * 1024
WIDE = ("y", "z")
NARROW = ("x", "core")


def rms_scale(values, gain):
    wide = values.astype(jnp.float32)
    power = jnp.mean(wide * wide, axis=-1, keepdims=True)
    return (wide * lax.rsqrt(power + epsilon) * gain.astype(jnp.float32)).astype(jnp.bfloat16)


def dot_t(left, right):
    return lax.dot_general(
        left, right, (((1,), (1,)), ((), ())), preferred_element_type=jnp.float32
    )


def spread(values, axis):
    copies = jnp.broadcast_to(values[None], (lax.axis_size(axis),) + values.shape)
    return lax.all_to_all(copies, axis, 0, 0)


def swap_cores(values):
    return lax.ppermute(values, "core", [(0, 1), (1, 0)])


def along_x(values, step):
    n_x = lax.axis_size("x")
    pairs = [
        (2 * x + core, 2 * ((x + step * (1 - 2 * core)) % n_x) + core)
        for x in range(n_x)
        for core in range(2)
    ]
    return lax.ppermute(values, NARROW, pairs)


def load(source, target, sem):
    copy = pltpu.make_async_copy(source, target, sem)
    copy.start()
    return copy


def first_kernel(wq_ref, wkv_ref, wo_ref, copies_ref, sems):
    at, loads = 0, []
    for k, ref in enumerate((wq_ref, wkv_ref, wo_ref)):
        columns = ref.shape[1]
        loads.append(load(ref, copies_ref.at[0, :, pl.ds(at, columns)], sems.at[k]))
        at += columns
    for copy in loads:
        copy.wait()
    for k in range(1, copies_ref.shape[0]):
        copies_ref[k] = copies_ref[0]


def message_kernel(states_ref, message_ref, tail_ref, sem):
    tail = tail_ref.shape[0]
    load(states_ref.at[pl.ds(TXT - tail, tail)], tail_ref, sem).wait()
    row = tail_ref[...].astype(jnp.float32)[-1:]
    pieces, share = message_ref.shape[1:]
    tile = jnp.concatenate([row[:, j * share : (j + 1) * share] for j in range(pieces)], axis=0)
    for k in range(message_ref.shape[0]):
        message_ref[k] = tile


def probe_kernel(gain_ref, last_ref, wq_ref, wkv_ref, probes_ref, raw_ref):
    raw = jnp.concatenate([last_ref[:, j, :] for j in range(last_ref.shape[1])], axis=1)
    raw_ref[...] = raw
    power = jnp.mean(raw * raw, axis=-1, keepdims=True)
    normed = raw * lax.rsqrt(power + epsilon) * gain_ref[...].astype(jnp.float32)
    queries = jnp.dot(normed.astype(jnp.bfloat16), wq_ref[...], preferred_element_type=jnp.float32)
    queries = queries.astype(jnp.bfloat16)
    keys = wkv_ref[:, :HEAD_DIM]
    for head in range(probes_ref.shape[1]):
        lanes = slice(head * HEAD_DIM, (head + 1) * HEAD_DIM)
        probes_ref[:, head, :] = dot_t(queries[:, lanes], keys).astype(jnp.bfloat16)


def pool_kernel(probes_ref, normed_ref, pooled_ref):
    items, per = probes_ref.shape[:2]
    probes = jnp.concatenate([probes_ref[k].astype(jnp.float32) for k in range(items)], axis=0)
    scores = dot_t(probes.astype(jnp.bfloat16), normed_ref[...]) * (1.0 / math.sqrt(HEAD_DIM))
    parts = jnp.exp(scores - jnp.max(scores, axis=1, keepdims=True))
    parts = parts / jnp.sum(parts, axis=1, keepdims=True)
    pooled = jnp.dot(parts.astype(jnp.bfloat16), normed_ref[...], preferred_element_type=jnp.float32)
    for k in range(items):
        pooled_ref[k] = pooled[k * per : (k + 1) * per].astype(jnp.bfloat16)


def embed_kernel(gain_ref, terms_ref, last_ref, embedded_ref, normed_ref):
    total = last_ref[...]
    for k in range(terms_ref.shape[0]):
        total = total + terms_ref[k].astype(jnp.float32)
    embedded = total.astype(jnp.bfloat16)
    embedded_ref[...] = embedded
    wide = embedded.astype(jnp.float32)
    power = jnp.mean(wide * wide, axis=-1, keepdims=True)
    normed = wide * lax.rsqrt(power + epsilon) * gain_ref[...].astype(jnp.float32)
    normed_ref[...] = normed.astype(jnp.bfloat16)


def layout_kernel(scalar_ref, weights_ref, theirs_ref, mine_ref):
    n_x, share, out_width = mine_ref.shape
    core, place = scalar_ref[1], scalar_ref[2]
    step = 1 - 2 * core
    for k, (theirs, mine) in enumerate(((2, 2), (step, -step), (-step, step), (0, 0))):
        rows = (2 * lax.rem(place + n_x + theirs, n_x) + 1 - core) * share
        rows = pl.ds(pl.multiple_of(rows, share), share)
        theirs_ref[k] = weights_ref[rows, -out_width:]
        rows = (2 * lax.rem(place + n_x + mine, n_x) + core) * share
        rows = pl.ds(pl.multiple_of(rows, share), share)
        mine_ref[k] = weights_ref[rows, -out_width:]


def one_hot(places_ref, slots, catalog):
    every = lax.broadcasted_iota(jnp.int32, (slots, catalog), 1)
    return jnp.where(places_ref[...] == every, 1.0, 0.0).astype(jnp.bfloat16)


def residual_kernel(places_ref, catalog_ref, mixed_ref, residual_ref):
    del mixed_ref
    slots, share = residual_ref.shape
    picks = one_hot(places_ref, slots, catalog_ref.shape[0])
    residual_ref[...] = jnp.dot(
        picks, catalog_ref[:, -share:], preferred_element_type=jnp.float32
    ).astype(jnp.bfloat16)


def user_kernel(
    scalar_ref, places_ref, catalog_ref, mixed_ref, query_ref, key_ref, value_ref
):
    length = scalar_ref[0]
    slots, q_width = mixed_ref.shape
    catalog, kv_at = catalog_ref.shape[0], q_width + 2 * HEAD_DIM
    picks = one_hot(places_ref, slots, catalog)
    picked = jnp.dot(picks, catalog_ref[:, :kv_at], preferred_element_type=jnp.float32)
    scale = 1.0 / math.sqrt(HEAD_DIM)
    heads = q_width // HEAD_DIM
    for head in range(heads):
        lanes = slice(head * HEAD_DIM, (head + 1) * HEAD_DIM)
        query_ref[head] = (picked[:, lanes] * scale).astype(jnp.bfloat16)
    key_ref[...] = picked[:, q_width : q_width + HEAD_DIM].astype(jnp.bfloat16)
    values = picked[:, q_width + HEAD_DIM : kv_at]
    value_ref[...] = jnp.concatenate([values, jnp.ones_like(values)], axis=1).astype(jnp.bfloat16)
    chunk = min(slots, 256)
    for start in range(0, slots, chunk):
        upto = start + chunk
        row = start + lax.broadcasted_iota(jnp.int32, (chunk, upto), 0)
        column = lax.broadcasted_iota(jnp.int32, (chunk, upto), 1)
        allowed = (column <= row) & (column < length)
        queries = query_ref[:, start:upto, :].reshape(heads * chunk, HEAD_DIM)
        scores = dot_t(queries, key_ref[:upto, :]).reshape(heads, chunk, upto)
        scores = jnp.where(allowed[None], scores, -1e30)
        parts = jnp.exp(scores - jnp.max(scores, axis=2, keepdims=True)).astype(jnp.bfloat16)
        mixed = jnp.dot(
            parts.reshape(heads * chunk, upto),
            value_ref[:upto, :],
            preferred_element_type=jnp.float32,
        )
        mixed = (mixed[:, :HEAD_DIM] / mixed[:, HEAD_DIM:]).astype(jnp.bfloat16)
        for head in range(heads):
            lanes = slice(head * HEAD_DIM, (head + 1) * HEAD_DIM)
            mixed_ref[start:upto, lanes] = mixed[head * chunk : (head + 1) * chunk]


def output_kernel(mine_ref, others_ref, wo_mine_ref, wo_others_ref, *block_refs):
    skip = wo_mine_ref.shape[0] - len(block_refs)
    for k, ref in enumerate(block_refs):
        terms = dot_t(mine_ref[...], wo_mine_ref[skip + k])
        terms += dot_t(others_ref[...], wo_others_ref[skip + k])
        ref[...] = terms.astype(jnp.bfloat16)


def first_output_kernel(mine_ref, others_ref, wo_mine_ref, wo_others_ref, block_ref):
    terms = dot_t(mine_ref[...], wo_mine_ref[0]) + dot_t(others_ref[...], wo_others_ref[0])
    block_ref[...] = terms.astype(jnp.bfloat16)


SMEM = pl.BlockSpec(memory_space=pltpu.SMEM)
VMEM = pl.BlockSpec(memory_space=pltpu.VMEM)
ANY = pl.BlockSpec(memory_space=pl.ANY)


def call(kernel, name, limit, outs, in_specs, ins, scratch=()):
    return pl.pallas_call(
        kernel,
        name=name,
        out_shape=outs,
        in_specs=in_specs,
        out_specs=jax.tree.map(lambda _: VMEM, outs),
        scratch_shapes=scratch,
        compiler_params=pltpu.CompilerParams(vmem_limit_bytes=limit * MIB),
    )(*ins)


def local(
    item_states,
    item_gain,
    wq_item,
    wkv_item,
    wo_item,
    user_gain,
    wq_user,
    wkv_user,
    wo_user,
    history_items,
    history_lengths,
):
    width = item_states.shape[1]
    n_x = lax.axis_size("x")
    n_narrow = 2 * n_x
    share = width // n_narrow
    core = lax.axis_index("core")
    me = lax.axis_index("x") * 2 + core
    scale = 1.0 / math.sqrt(HEAD_DIM)

    columns = wq_user.shape[1] + 2 * HEAD_DIM + wo_user.shape[0]
    n_z = lax.axis_size("z")
    depth, heads_width = wq_user.shape
    kv_at = heads_width + 2 * HEAD_DIM
    columns = kv_at + wo_user.shape[0]
    copies = call(
        first_kernel,
        "user_weights",
        60,
        jax.ShapeDtypeStruct((n_z, depth, columns), jnp.bfloat16),
        [ANY] * 3,
        (wq_user, wkv_user.reshape(depth, -1), wo_user.T),
        [pltpu.SemaphoreType.DMA((3,))],
    )
    weights_z = lax.all_to_all(copies, "z", 0, 0).reshape(n_z * depth, columns)
    messages = call(
        message_kernel,
        "last_rows",
        20,
        jax.ShapeDtypeStruct((n_narrow, n_narrow, share), jnp.float32),
        [ANY],
        (item_states,),
        [pltpu.VMEM((16, width), jnp.bfloat16), pltpu.SemaphoreType.DMA],
    )
    length = history_lengths[0]
    weights_z, messages, normed, places, scalars, gain_row, item_gain_row = (
        lax.optimization_barrier(
            (
                weights_z,
                messages,
                rms_scale(item_states, item_gain),
                history_items[0][:, None],
                jnp.stack([length, core, lax.axis_index("x")]).astype(jnp.int32),
                user_gain[None],
                item_gain[None],
            )
        )
    )
    weights_all = lax.all_gather(weights_z, "y", axis=0, tiled=True)
    last_raw = lax.all_to_all(messages, NARROW, 0, 0)
    per = wq_item.shape[1] // HEAD_DIM
    wkv = wkv_item.reshape(width, -1)
    wv = wkv[:, HEAD_DIM:]
    probes, last_raw = call(
        probe_kernel,
        "item_probes",
        20,
        (
            jax.ShapeDtypeStruct((n_narrow, per, width), jnp.bfloat16),
            jax.ShapeDtypeStruct((n_narrow, width), jnp.float32),
        ),
        [VMEM] * 4,
        (item_gain_row, last_raw, wq_item, wkv),
    )
    probes = lax.all_to_all(probes, NARROW, 0, 0)
    pooled = call(
        pool_kernel,
        "item_attention",
        20,
        jax.ShapeDtypeStruct(probes.shape, jnp.bfloat16),
        [VMEM] * 2,
        (probes, normed),
    )
    pooled = lax.all_to_all(pooled, NARROW, 0, 0)
    mixed = jnp.dot(pooled.reshape(-1, width), wv, preferred_element_type=jnp.float32)
    mixed = mixed.astype(jnp.bfloat16).reshape(n_narrow, -1)
    partial_sum = jnp.dot(mixed, wo_item, preferred_element_type=jnp.float32)
    terms = spread(partial_sum.astype(jnp.bfloat16), NARROW)
    group = terms.shape[1]
    embedded, items_normed = call(
        embed_kernel,
        "item_embeddings",
        20,
        [jax.ShapeDtypeStruct((group, width), jnp.bfloat16)] * 2,
        [VMEM] * 3,
        (gain_row, terms, last_raw),
    )
    item_part = lax.dynamic_slice_in_dim(embedded, me * share, share, 1)
    projected = jnp.dot(
        items_normed, weights_all[:, :kv_at], preferred_element_type=jnp.float32
    ).astype(jnp.bfloat16)
    projected = jnp.concatenate([projected, item_part], axis=1)

    catalog = spread(projected, WIDE).reshape(-1, kv_at + share)

    wo_theirs, wo_mine = call(
        layout_kernel,
        "output_weights",
        20,
        [jax.ShapeDtypeStruct((n_x, share, wo_user.shape[0]), jnp.bfloat16)] * 2,
        [SMEM, VMEM],
        (scalars, weights_all),
    )
    wo_others = swap_cores(wo_theirs)
    slots = history_items.shape[1]
    user_mixed = call(
        user_kernel,
        "user_attention",
        20,
        jax.ShapeDtypeStruct((slots, heads_width), jnp.bfloat16),
        [SMEM] + [VMEM] * 2,
        (scalars, places, catalog),
        [
            pltpu.VMEM((per, slots, HEAD_DIM), jnp.bfloat16),
            pltpu.VMEM((slots, HEAD_DIM), jnp.bfloat16),
            pltpu.VMEM((slots, 2 * HEAD_DIM), jnp.bfloat16),
        ],
    )

    residual = call(
        residual_kernel,
        "residual_rows",
        20,
        jax.ShapeDtypeStruct((slots, share), jnp.bfloat16),
        [VMEM] * 3,
        (places, catalog, user_mixed),
    )

    block = jax.ShapeDtypeStruct((slots, share), jnp.bfloat16)
    operands = (user_mixed, swap_cores(user_mixed), wo_mine, wo_others)
    first = call(first_output_kernel, "output_first", 20, block, [VMEM] * 4, operands)
    direct, second, own = call(
        output_kernel, "output_blocks", 20, [block] * (n_x - 1), [VMEM] * 4, operands
    )
    relay = along_x(first, 1)
    direct = along_x(direct, -1)
    relay = (relay.astype(jnp.float32) + second.astype(jnp.float32)).astype(jnp.bfloat16)
    relay = along_x(relay, 1)
    live = (jnp.arange(slots, dtype=jnp.int32) < length)[:, None]
    summed = residual.astype(jnp.float32) + own.astype(jnp.float32) + direct.astype(jnp.float32)
    summed = lax.optimization_barrier(summed) + relay.astype(jnp.float32)
    user_states = jnp.where(live, summed, 0.0).astype(jnp.bfloat16)
    return (item_part, user_states)


def solution(mesh):
    n_wide, n_narrow = mesh.shape["wide"], mesh.shape["narrow"]
    side = math.isqrt(n_wide)
    fine = Mesh(
        mesh.devices.reshape(side, n_wide // side, n_narrow // 2, 2), WIDE + NARROW
    )
    return jax.shard_map(
        local,
        mesh=fine,
        in_specs=(
            P(WIDE + NARROW, None),
            P(),
            P(None, NARROW),
            P(None, NARROW, None),
            P(NARROW, None),
            P(),
            P(WIDE, NARROW),
            P(WIDE, NARROW, None),
            P(NARROW, WIDE),
            P(WIDE, None),
            P(WIDE),
        ),
        out_specs=(P(WIDE, NARROW), P(WIDE, NARROW)),
        check_vma=False,
    )
```

```python
import math

import jax
import jax.numpy as jnp
from jax import lax
from jax.experimental import pallas as pl
from jax.experimental.pallas import tpu as pltpu
from jax.sharding import Mesh
from jax.sharding import PartitionSpec as P

HEAD_DIM = 64
TXT = 128
epsilon = 1e-05
MIB = 1024 * 1024
WIDE = ("y", "z")
NARROW = ("x", "core")


def rms_scale(values, gain):
    wide = values.astype(jnp.float32)
    power = jnp.mean(wide * wide, axis=-1, keepdims=True)
    return (wide * lax.rsqrt(power + epsilon) * gain.astype(jnp.float32)).astype(jnp.bfloat16)


def dot_t(left, right):
    return lax.dot_general(
        left, right, (((1,), (1,)), ((), ())), preferred_element_type=jnp.float32
    )


def spread(values, axis):
    copies = jnp.broadcast_to(values[None], (lax.axis_size(axis),) + values.shape)
    return lax.all_to_all(copies, axis, 0, 0)


def swap_cores(values):
    return lax.ppermute(values, "core", [(0, 1), (1, 0)])


def along_x(values, step):
    n_x = lax.axis_size("x")
    pairs = [
        (2 * x + core, 2 * ((x + step * (1 - 2 * core)) % n_x) + core)
        for x in range(n_x)
        for core in range(2)
    ]
    return lax.ppermute(values, NARROW, pairs)


def load(source, target, sem):
    copy = pltpu.make_async_copy(source, target, sem)
    copy.start()
    return copy


def first_kernel(wq_ref, wkv_ref, wo_ref, copies_ref, sems):
    at, loads = 0, []
    for k, ref in enumerate((wq_ref, wkv_ref, wo_ref)):
        columns = ref.shape[1]
        loads.append(load(ref, copies_ref.at[0, :, pl.ds(at, columns)], sems.at[k]))
        at += columns
    for copy in loads:
        copy.wait()
    for k in range(1, copies_ref.shape[0]):
        copies_ref[k] = copies_ref[0]


def message_kernel(states_ref, message_ref, tail_ref, sem):
    tail = tail_ref.shape[0]
    load(states_ref.at[pl.ds(TXT - tail, tail)], tail_ref, sem).wait()
    row = tail_ref[...].astype(jnp.float32)[-1:]
    pieces, share = message_ref.shape[1:]
    tile = jnp.concatenate([row[:, j * share : (j + 1) * share] for j in range(pieces)], axis=0)
    for k in range(message_ref.shape[0]):
        message_ref[k] = tile


def probe_kernel(gain_ref, last_ref, wq_ref, wkv_ref, probes_ref, raw_ref):
    raw = jnp.concatenate([last_ref[:, j, :] for j in range(last_ref.shape[1])], axis=1)
    raw_ref[...] = raw
    power = jnp.mean(raw * raw, axis=-1, keepdims=True)
    normed = raw * lax.rsqrt(power + epsilon) * gain_ref[...].astype(jnp.float32)
    queries = jnp.dot(normed.astype(jnp.bfloat16), wq_ref[...], preferred_element_type=jnp.float32)
    queries = queries.astype(jnp.bfloat16)
    keys = wkv_ref[:, :HEAD_DIM]
    for head in range(probes_ref.shape[1]):
        lanes = slice(head * HEAD_DIM, (head + 1) * HEAD_DIM)
        probes_ref[:, head, :] = dot_t(queries[:, lanes], keys).astype(jnp.bfloat16)


def pool_kernel(probes_ref, normed_ref, pooled_ref):
    items, per = probes_ref.shape[:2]
    probes = jnp.concatenate([probes_ref[k].astype(jnp.float32) for k in range(items)], axis=0)
    scores = dot_t(probes.astype(jnp.bfloat16), normed_ref[...]) * (1.0 / math.sqrt(HEAD_DIM))
    parts = jnp.exp(scores - jnp.max(scores, axis=1, keepdims=True))
    parts = parts / jnp.sum(parts, axis=1, keepdims=True)
    pooled = jnp.dot(parts.astype(jnp.bfloat16), normed_ref[...], preferred_element_type=jnp.float32)
    for k in range(items):
        pooled_ref[k] = pooled[k * per : (k + 1) * per].astype(jnp.bfloat16)


def embed_kernel(gain_ref, terms_ref, last_ref, embedded_ref, normed_ref):
    total = last_ref[...]
    for k in range(terms_ref.shape[0]):
        total = total + terms_ref[k].astype(jnp.float32)
    embedded = total.astype(jnp.bfloat16)
    embedded_ref[...] = embedded
    wide = embedded.astype(jnp.float32)
    power = jnp.mean(wide * wide, axis=-1, keepdims=True)
    normed = wide * lax.rsqrt(power + epsilon) * gain_ref[...].astype(jnp.float32)
    normed_ref[...] = normed.astype(jnp.bfloat16)


def layout_kernel(scalar_ref, weights_ref, theirs_ref, mine_ref):
    n_x, share, out_width = mine_ref.shape
    core, place = scalar_ref[1], scalar_ref[2]
    step = 1 - 2 * core
    for k, (theirs, mine) in enumerate(((2, 2), (step, -step), (-step, step), (0, 0))):
        rows = (2 * lax.rem(place + n_x + theirs, n_x) + 1 - core) * share
        rows = pl.ds(pl.multiple_of(rows, share), share)
        theirs_ref[k] = weights_ref[rows, -out_width:]
        rows = (2 * lax.rem(place + n_x + mine, n_x) + core) * share
        rows = pl.ds(pl.multiple_of(rows, share), share)
        mine_ref[k] = weights_ref[rows, -out_width:]


def one_hot(places_ref, slots, catalog):
    every = lax.broadcasted_iota(jnp.int32, (slots, catalog), 1)
    return jnp.where(places_ref[...] == every, 1.0, 0.0).astype(jnp.bfloat16)


def residual_kernel(places_ref, catalog_ref, mixed_ref, residual_ref):
    del mixed_ref
    slots, share = residual_ref.shape
    picks = one_hot(places_ref, slots, catalog_ref.shape[0])
    residual_ref[...] = jnp.dot(
        picks, catalog_ref[:, -share:], preferred_element_type=jnp.float32
    ).astype(jnp.bfloat16)


def user_kernel(
    scalar_ref, places_ref, catalog_ref, mixed_ref, query_ref, key_ref, value_ref
):
    length = scalar_ref[0]
    slots, q_width = mixed_ref.shape
    catalog, kv_at = catalog_ref.shape[0], q_width + 2 * HEAD_DIM
    picks = one_hot(places_ref, slots, catalog)
    picked = jnp.dot(picks, catalog_ref[:, :kv_at], preferred_element_type=jnp.float32)
    scale = 1.0 / math.sqrt(HEAD_DIM)
    heads = q_width // HEAD_DIM
    for head in range(heads):
        lanes = slice(head * HEAD_DIM, (head + 1) * HEAD_DIM)
        query_ref[head] = (picked[:, lanes] * scale).astype(jnp.bfloat16)
    key_ref[...] = picked[:, q_width : q_width + HEAD_DIM].astype(jnp.bfloat16)
    values = picked[:, q_width + HEAD_DIM : kv_at]
    value_ref[...] = jnp.concatenate([values, jnp.ones_like(values)], axis=1).astype(jnp.bfloat16)
    chunk = min(slots, 128)
    for start in range(0, slots, chunk):
        upto = start + chunk
        row = start + lax.broadcasted_iota(jnp.int32, (chunk, upto), 0)
        column = lax.broadcasted_iota(jnp.int32, (chunk, upto), 1)
        allowed = (column <= row) & (column < length)
        queries = query_ref[:, start:upto, :].reshape(heads * chunk, HEAD_DIM)
        scores = dot_t(queries, key_ref[:upto, :]).reshape(heads, chunk, upto)
        scores = jnp.where(allowed[None], scores, -1e30)
        parts = jnp.exp(scores - jnp.max(scores, axis=2, keepdims=True)).astype(jnp.bfloat16)
        mixed = jnp.dot(
            parts.reshape(heads * chunk, upto),
            value_ref[:upto, :],
            preferred_element_type=jnp.float32,
        )
        mixed = (mixed[:, :HEAD_DIM] / mixed[:, HEAD_DIM:]).astype(jnp.bfloat16)
        for head in range(heads):
            lanes = slice(head * HEAD_DIM, (head + 1) * HEAD_DIM)
            mixed_ref[start:upto, lanes] = mixed[head * chunk : (head + 1) * chunk]


def output_kernel(mine_ref, others_ref, wo_mine_ref, wo_others_ref, *block_refs):
    skip = wo_mine_ref.shape[0] - len(block_refs)
    for k, ref in enumerate(block_refs):
        terms = dot_t(mine_ref[...], wo_mine_ref[skip + k])
        terms += dot_t(others_ref[...], wo_others_ref[skip + k])
        ref[...] = terms.astype(jnp.bfloat16)


def first_output_kernel(mine_ref, others_ref, wo_mine_ref, wo_others_ref, block_ref):
    terms = dot_t(mine_ref[...], wo_mine_ref[0]) + dot_t(others_ref[...], wo_others_ref[0])
    block_ref[...] = terms.astype(jnp.bfloat16)


SMEM = pl.BlockSpec(memory_space=pltpu.SMEM)
VMEM = pl.BlockSpec(memory_space=pltpu.VMEM)
ANY = pl.BlockSpec(memory_space=pl.ANY)


def call(kernel, name, limit, outs, in_specs, ins, scratch=()):
    return pl.pallas_call(
        kernel,
        name=name,
        out_shape=outs,
        in_specs=in_specs,
        out_specs=jax.tree.map(lambda _: VMEM, outs),
        scratch_shapes=scratch,
        compiler_params=pltpu.CompilerParams(vmem_limit_bytes=limit * MIB),
    )(*ins)


def local(
    item_states,
    item_gain,
    wq_item,
    wkv_item,
    wo_item,
    user_gain,
    wq_user,
    wkv_user,
    wo_user,
    history_items,
    history_lengths,
):
    width = item_states.shape[1]
    n_x = lax.axis_size("x")
    n_narrow = 2 * n_x
    share = width // n_narrow
    core = lax.axis_index("core")
    me = lax.axis_index("x") * 2 + core
    scale = 1.0 / math.sqrt(HEAD_DIM)

    columns = wq_user.shape[1] + 2 * HEAD_DIM + wo_user.shape[0]
    n_z = lax.axis_size("z")
    depth, heads_width = wq_user.shape
    kv_at = heads_width + 2 * HEAD_DIM
    columns = kv_at + wo_user.shape[0]
    copies = call(
        first_kernel,
        "user_weights",
        60,
        jax.ShapeDtypeStruct((n_z, depth, columns), jnp.bfloat16),
        [ANY] * 3,
        (wq_user, wkv_user.reshape(depth, -1), wo_user.T),
        [pltpu.SemaphoreType.DMA((3,))],
    )
    weights_z = lax.all_to_all(copies, "z", 0, 0).reshape(n_z * depth, columns)
    messages = call(
        message_kernel,
        "last_rows",
        20,
        jax.ShapeDtypeStruct((n_narrow, n_narrow, share), jnp.float32),
        [ANY],
        (item_states,),
        [pltpu.VMEM((16, width), jnp.bfloat16), pltpu.SemaphoreType.DMA],
    )
    length = history_lengths[0]
    weights_z, messages, normed, places, scalars, gain_row, item_gain_row = (
        lax.optimization_barrier(
            (
                weights_z,
                messages,
                rms_scale(item_states, item_gain),
                history_items[0][:, None],
                jnp.stack([length, core, lax.axis_index("x")]).astype(jnp.int32),
                user_gain[None],
                item_gain[None],
            )
        )
    )
    weights_all = lax.all_gather(weights_z, "y", axis=0, tiled=True)
    last_raw = lax.all_to_all(messages, NARROW, 0, 0)
    per = wq_item.shape[1] // HEAD_DIM
    wkv = wkv_item.reshape(width, -1)
    wv = wkv[:, HEAD_DIM:]
    probes, last_raw = call(
        probe_kernel,
        "item_probes",
        20,
        (
            jax.ShapeDtypeStruct((n_narrow, per, width), jnp.bfloat16),
            jax.ShapeDtypeStruct((n_narrow, width), jnp.float32),
        ),
        [VMEM] * 4,
        (item_gain_row, last_raw, wq_item, wkv),
    )
    probes = lax.all_to_all(probes, NARROW, 0, 0)
    pooled = call(
        pool_kernel,
        "item_attention",
        20,
        jax.ShapeDtypeStruct(probes.shape, jnp.bfloat16),
        [VMEM] * 2,
        (probes, normed),
    )
    pooled = lax.all_to_all(pooled, NARROW, 0, 0)
    mixed = jnp.dot(pooled.reshape(-1, width), wv, preferred_element_type=jnp.float32)
    mixed = mixed.astype(jnp.bfloat16).reshape(n_narrow, -1)
    partial_sum = jnp.dot(mixed, wo_item, preferred_element_type=jnp.float32)
    terms = spread(partial_sum.astype(jnp.bfloat16), NARROW)
    group = terms.shape[1]
    embedded, items_normed = call(
        embed_kernel,
        "item_embeddings",
        20,
        [jax.ShapeDtypeStruct((group, width), jnp.bfloat16)] * 2,
        [VMEM] * 3,
        (gain_row, terms, last_raw),
    )
    item_part = lax.dynamic_slice_in_dim(embedded, me * share, share, 1)
    projected = jnp.dot(
        items_normed, weights_all[:, :kv_at], preferred_element_type=jnp.float32
    ).astype(jnp.bfloat16)
    projected = jnp.concatenate([projected, item_part], axis=1)

    catalog = spread(projected, WIDE).reshape(-1, kv_at + share)

    wo_theirs, wo_mine = call(
        layout_kernel,
        "output_weights",
        20,
        [jax.ShapeDtypeStruct((n_x, share, wo_user.shape[0]), jnp.bfloat16)] * 2,
        [SMEM, VMEM],
        (scalars, weights_all),
    )
    wo_others = swap_cores(wo_theirs)
    slots = history_items.shape[1]
    user_mixed = call(
        user_kernel,
        "user_attention",
        20,
        jax.ShapeDtypeStruct((slots, heads_width), jnp.bfloat16),
        [SMEM] + [VMEM] * 2,
        (scalars, places, catalog),
        [
            pltpu.VMEM((per, slots, HEAD_DIM), jnp.bfloat16),
            pltpu.VMEM((slots, HEAD_DIM), jnp.bfloat16),
            pltpu.VMEM((slots, 2 * HEAD_DIM), jnp.bfloat16),
        ],
    )

    residual = call(
        residual_kernel,
        "residual_rows",
        20,
        jax.ShapeDtypeStruct((slots, share), jnp.bfloat16),
        [VMEM] * 3,
        (places, catalog, user_mixed),
    )

    block = jax.ShapeDtypeStruct((slots, share), jnp.bfloat16)
    operands = (user_mixed, swap_cores(user_mixed), wo_mine, wo_others)
    first = call(first_output_kernel, "output_first", 20, block, [VMEM] * 4, operands)
    direct, second, own = call(
        output_kernel, "output_blocks", 20, [block] * (n_x - 1), [VMEM] * 4, operands
    )
    relay = along_x(first, 1)
    direct = along_x(direct, -1)
    relay = (relay.astype(jnp.float32) + second.astype(jnp.float32)).astype(jnp.bfloat16)
    relay = along_x(relay, 1)
    live = (jnp.arange(slots, dtype=jnp.int32) < length)[:, None]
    summed = residual.astype(jnp.float32) + own.astype(jnp.float32) + direct.astype(jnp.float32)
    summed = lax.optimization_barrier(summed) + relay.astype(jnp.float32)
    user_states = jnp.where(live, summed, 0.0).astype(jnp.bfloat16)
    return (item_part, user_states)


def solution(mesh):
    n_wide, n_narrow = mesh.shape["wide"], mesh.shape["narrow"]
    side = math.isqrt(n_wide)
    fine = Mesh(
        mesh.devices.reshape(side, n_wide // side, n_narrow // 2, 2), WIDE + NARROW
    )
    return jax.shard_map(
        local,
        mesh=fine,
        in_specs=(
            P(WIDE + NARROW, None),
            P(),
            P(None, NARROW),
            P(None, NARROW, None),
            P(NARROW, None),
            P(),
            P(WIDE, NARROW),
            P(WIDE, NARROW, None),
            P(NARROW, WIDE),
            P(WIDE, None),
            P(WIDE),
        ),
        out_specs=(P(WIDE, NARROW), P(WIDE, NARROW)),
        check_vma=False,
    )
```
